256 devices in a mesh: dom: 32 (over y, z), sub: 8 (over x, core).
Axes of the slice: x: 4, y: 4, z: 8, core: 2. Of those that a mesh axis runs over, the one named last changes fastest.
Arguments:
- velocity: float32 [3, 216, 32768], P(None, None, ('dom', 'sub')), may hold values from -5 to 5
- base_flow: float32 [3, 216, 32768], P(None, None, ('dom', 'sub')), may hold values from -1.5 to 1.5
- viscosity: float32 [216, 32768], P(None, ('dom', 'sub')), may hold values from 0.05 to 1
- cell_order: int32 [256, 128], P(('dom', 'sub')), may hold values from 0 to 127, each once within a row
- coarse_inv: float32 [256, 256], replicated, as said below
Outputs:
- linearized: float32 [3, 216, 32768], P(None, None, ('dom', 'sub'))
- pressure: float32 [216, 32768], P(None, ('dom', 'sub'))
The draws below stay inside these ranges and needn't reach their ends.
Inputs may be any that keep to these rules, and one draw needn't show every extreme that they name: `cell_order`: row d gives, for each of the 128 element slots of block d in order, that element's cell within the block; each cell once. `coarse_inv`: symmetric positive definite.
All inputs are finite; a program needn't handle non-finite values.
Results may differ from the reference program's by a relative error of at most 0.0003.
Values sent between devices are 32-bit elements; how exact they have to be, the bound alone decides.
A program may use at most 64 MiB of HBM per device.

```python
import math
import jax
import jax.numpy as jnp
import numpy as np
from jax import lax

ELX = 2
ELY = 2
ELZ = 32
ITERS = 3
E_DEV = 128
XBLOCKS = 32
YBLOCKS = 8
NCOARSE = 256
NE = 32768
NGX = 321
NGY = 81
NGZ = 161


def draw_velocity(key, part):
    key = jax.random.fold_in(key, 11)
    element = jnp.arange(NE)
    column = (element // (E_DEV * YBLOCKS)).astype(jnp.float32) / (XBLOCKS - 1)
    growth = 3.0 ** column
    values = jnp.clip(jax.random.normal(key, (3, 216, NE), jnp.float32), -4.0, 4.0) * 0.3
    return values * growth[None, None, :]


def draw_coarse_inv(key, part):
    key = jax.random.fold_in(key, 23)
    key_scale, key_shift = jax.random.split(key)
    reach = 1.0 / 3.0
    low_scale = 0.7
    high_scale = 1.4
    block_ids = jnp.arange(NCOARSE)
    column = (block_ids // YBLOCKS).astype(jnp.float32)
    row = (block_ids % YBLOCKS).astype(jnp.float32)
    apart_x = jnp.abs(column[:, None] - column[None, :])
    apart_y = jnp.abs(row[:, None] - row[None, :])
    kernel = jnp.exp(-apart_x / (reach * XBLOCKS) - apart_y / (reach * YBLOCKS))
    scales = jnp.exp(jax.random.uniform(key_scale, (NCOARSE,), jnp.float32, jnp.log(low_scale), jnp.log(high_scale)))
    shift = jax.random.uniform(key_shift, (NCOARSE,), jnp.float32, 0.2, 0.6) * scales * scales
    overall = 4.0 / (2.0 * E_DEV * jnp.sqrt(jnp.float32(NCOARSE)))
    matrix = scales[:, None] * kernel * scales[None, :] + jnp.diag(shift)
    return overall * matrix


def block_levels(stream_key, shape, shards, low, largest):
    def one(axis_at, parts):
        heights = jax.random.uniform(jax.random.fold_in(jax.random.fold_in(stream_key, 6), axis_at), (parts,), jnp.float32, low / len(shards), largest / len(shards))
        return jnp.repeat(jnp.exp(heights), shape[axis_at] // parts).reshape((-1,) + (1,) * (len(shape) - axis_at - 1))

    factor_of = one(*shards[0])
    for cut in shards[1:]:
        factor_of = factor_of * one(*cut)
    return factor_of


def centred(stream_key, shape, scale, most, shards=(), kind=jnp.bfloat16):
    entries = scale * jax.random.normal(stream_key, shape, jnp.float32)
    if shards:
        entries = entries * block_levels(stream_key, shape, shards, -0.22, 0.18)
    return jnp.clip(entries, -most, most).astype(kind)


def setup_inputs(seed: int = 0) -> dict:
    splits = jax.random.split(jax.random.key(seed), 6)
    velocity = draw_velocity(jax.random.fold_in(splits[5], 71), 0)
    base_flow = centred(splits[1], (3, 216, NE), 0.3, 1.5, ((2, 256),), jnp.float32)
    viscosity = jnp.clip(jnp.exp(math.log(1.0) - 2.9957323 * jax.random.uniform(splits[2], (216, NE), jnp.float32) ** block_levels(splits[2], (216, NE), ((1, 256),), -0.2, 0.2)), 0.05, 1.0)
    cell_order = jax.vmap(lambda own: jax.random.permutation(own, E_DEV))(jax.random.split(splits[3], NCOARSE)).reshape((NCOARSE, E_DEV)).astype(jnp.int32)
    coarse_inv = draw_coarse_inv(jax.random.fold_in(splits[5], 71), 0)
    return dict(velocity=velocity, base_flow=base_flow, viscosity=viscosity, cell_order=cell_order, coarse_inv=coarse_inv)


PRECISE = lax.Precision.HIGHEST
REACTION = 0.001


def gll_tables():
    gll_points = np.array([-1.0, -0.7650553239294647, -0.2852315164806451, 0.2852315164806451, 0.7650553239294647, 1.0])
    gll_weights = np.array([1.0 / 15.0, 0.378474956297847, 0.5548583770354862, 0.5548583770354862, 0.378474956297847, 1.0 / 15.0])
    legendre = (63.0 * gll_points ** 5 - 70.0 * gll_points ** 3 + 15.0 * gll_points) / 8.0
    derivative = np.zeros((6, 6))
    for left_node in range(6):
        for right_node in range(6):
            if left_node != right_node:
                derivative[left_node, right_node] = legendre[left_node] / (legendre[right_node] * (gll_points[left_node] - gll_points[right_node]))
    derivative[0, 0] = -7.5
    derivative[5, 5] = 7.5
    mass_weights = gll_weights[:, None, None] * gll_weights[None, :, None] * gll_weights[None, None, :]
    return jnp.asarray(derivative, jnp.float32), jnp.asarray(mass_weights[..., None], jnp.float32)


def derive_along(values_in, dimension, matrix):
    einsum_forms = ("ai,...ijke->...ajke", "aj,...ijke->...iake", "ak,...ijke->...ijae")
    return jnp.einsum(einsum_forms[dimension], matrix, values_in, precision=PRECISE)


def derive_back(values_in, dimension, matrix):
    einsum_forms = ("ai,...ajke->...ijke", "aj,...iake->...ijke", "ak,...ijae->...ijke")
    return jnp.einsum(einsum_forms[dimension], matrix, values_in, precision=PRECISE)


def element_nodes(cell_order):
    block_ids = jnp.arange(XBLOCKS * YBLOCKS, dtype=jnp.int32)[:, None]
    column_block = block_ids // YBLOCKS
    row_block = block_ids % YBLOCKS
    element_x = (column_block * ELX + cell_order // (ELY * ELZ)).reshape(-1)
    element_y = (row_block * ELY + (cell_order // ELZ) % ELY).reshape(-1)
    element_z = (cell_order % ELZ).reshape(-1)
    offsets = jnp.arange(6, dtype=jnp.int32)
    node_x = 5 * element_x[None, None, None, :] + offsets[:, None, None, None]
    node_y = 5 * element_y[None, None, None, :] + offsets[None, :, None, None]
    node_z = 5 * element_z[None, None, None, :] + offsets[None, None, :, None]
    return ((node_x * NGY + node_y) * NGZ + node_z).astype(jnp.int32)


def membership(extent, width, blocks):
    coords = jnp.arange(extent, dtype=jnp.int32)[None, :]
    starts = width * jnp.arange(blocks, dtype=jnp.int32)[:, None]
    return ((coords >= starts) & (coords <= starts + width)).astype(jnp.float32)


def reference(velocity, base_flow, viscosity, cell_order, coarse_inv):
    derivative, mass_weights = gll_tables()
    node_ids = element_nodes(cell_order)
    flat_ids = node_ids.reshape(-1)
    node_total = NGX * NGY * NGZ

    def assemble(local_values):
        return jax.ops.segment_sum(local_values.reshape(-1), flat_ids, num_segments=node_total)

    moving = velocity.reshape(3, 6, 6, 6, NE)
    base_nodes = base_flow.reshape(3, 6, 6, 6, NE)
    advect_parts = []
    for component in range(3):
        accumulated = jnp.zeros((6, 6, 6, NE), jnp.float32)
        for dimension in range(3):
            accumulated = accumulated + base_nodes[dimension] * derive_along(moving[component], dimension, derivative)
            accumulated = accumulated + moving[dimension] * derive_along(base_nodes[component], dimension, derivative)
        advect_parts.append(-accumulated)
    advect = jnp.stack(advect_parts)
    divergence = derive_along(advect[0], 0, derivative) + derive_along(advect[1], 1, derivative) + derive_along(advect[2], 2, derivative)
    rhs = assemble(mass_weights * divergence)

    weighted = mass_weights * viscosity.reshape(6, 6, 6, NE)
    squared = derivative * derivative
    diag_local = REACTION * mass_weights + derive_back(weighted, 0, squared) + derive_back(weighted, 1, squared) + derive_back(weighted, 2, squared)
    inverse_diag = 1.0 / assemble(diag_local)

    def helmholtz(node_grid):
        local_values = node_grid[node_ids]
        result = REACTION * mass_weights * local_values
        for dimension in range(3):
            result = result + derive_back(weighted * derive_along(local_values, dimension, derivative), dimension, derivative)
        return assemble(result)

    member_x = membership(NGX, 5 * ELX, XBLOCKS)
    member_y = membership(NGY, 5 * ELY, YBLOCKS)
    coverage = member_x.sum(0)[:, None] * member_y.sum(0)[None, :]

    def precondition(residual):
        node_grid = residual.reshape(NGX, NGY, NGZ)
        column_sum = node_grid.sum(2) / coverage
        coarse_rhs = jnp.dot(jnp.dot(member_x, column_sum, precision=PRECISE), member_y.T, precision=PRECISE).reshape(-1)
        solved = jnp.dot(coarse_inv, coarse_rhs, precision=PRECISE).reshape(XBLOCKS, YBLOCKS)
        spread = jnp.dot(jnp.dot(member_x.T, solved, precision=PRECISE), member_y, precision=PRECISE) / coverage
        return residual * inverse_diag + jnp.broadcast_to(spread[:, :, None], (NGX, NGY, NGZ)).reshape(-1)

    pressure_grid = jnp.zeros((node_total,), jnp.float32)
    residual = rhs
    search = precondition(residual)
    direction = search
    current = jnp.sum(residual * search)
    for iteration in range(ITERS):
        applied = helmholtz(direction)
        step_size = current / jnp.sum(direction * applied)
        pressure_grid = pressure_grid + step_size * direction
        residual = residual - step_size * applied
        search = precondition(residual)
        following = jnp.sum(residual * search)
        direction = search + (following / current) * direction
        current = following

    pressure = pressure_grid[node_ids]
    gradient = jnp.stack([derive_along(pressure, dimension, derivative) for dimension in range(3)])
    linearized = (advect - gradient).reshape(3, 216, NE)
    return linearized, pressure.reshape(216, NE)
```

```python
import functools

import jax
import jax.numpy as jnp
import ml_dtypes
import numpy as np
from jax import lax
from jax.experimental import pallas as pl
from jax.experimental.pallas import tpu as pltpu
from jax.sharding import PartitionSpec as P

F32 = jnp.float32
BF16 = jnp.bfloat16
MESH = pl.DeviceIdType.MESH
REACTION = 0.001
DOM = 32
SUB = 8
ROWS = 224
NAT = 216
NFACE = 9


def gll_tables():
    points = np.array(
        [
            -1.0,
            -0.7650553239294647,
            -0.2852315164806451,
            0.2852315164806451,
            0.7650553239294647,
            1.0,
        ]
    )
    weights = np.array(
        [
            1.0 / 15.0,
            0.378474956297847,
            0.5548583770354862,
            0.5548583770354862,
            0.378474956297847,
            1.0 / 15.0,
        ]
    )
    legendre = (63.0 * points**5 - 70.0 * points**3 + 15.0 * points) / 8.0
    derivative = np.zeros((6, 6))
    for a in range(6):
        for b in range(6):
            if a != b:
                derivative[a, b] = legendre[a] / (legendre[b] * (points[a] - points[b]))
    derivative[0, 0] = -7.5
    derivative[5, 5] = 7.5
    mass = weights[:, None, None] * weights[None, :, None] * weights[None, None, :]
    return (
        derivative.astype(np.float32).astype(np.float64),
        mass.astype(np.float32).astype(np.float64).reshape(-1),
    )


def class_rows():
    mid = (1, 2, 3, 4)
    rows = [(i, j, k) for i in mid for j in mid for k in mid]
    for i in (0, 5):
        rows += [(i, j, k) for j in mid for k in mid]
        rows += [(i, j, k) for k in (0, 5) for j in mid]
        rows += [(i, j, k) for j in (0, 5) for k in mid]
        for j in (0, 5):
            for k in (0, 5):
                rows += [(i, j, k), None]
    for j in (0, 5):
        rows += [(i, j, k) for i in mid for k in mid]
        rows += [(i, j, k) for k in (0, 5) for i in mid]
    for k in (0, 5):
        rows += [(i, j, k) for i in mid for j in mid]
    return rows


def split_np(matrix):
    single = matrix.astype(np.float32)
    high = single.astype(ml_dtypes.bfloat16)
    low = (single - high.astype(np.float32)).astype(ml_dtypes.bfloat16)
    return high, low


def tables():
    derivative, mass = gll_tables()
    eye = np.eye(6)
    parts = [
        np.kron(np.kron(derivative, eye), eye),
        np.kron(np.kron(eye, derivative), eye),
        np.kron(np.kron(eye, eye), derivative),
    ]
    rows = class_rows()
    assert len(rows) == ROWS
    pick = np.zeros((ROWS, NAT))
    for at, node in enumerate(rows):
        if node is not None:
            pick[at, 36 * node[0] + 6 * node[1] + node[2]] = 1.0
    natural = np.zeros((3, ROWS, 256))
    from_class = np.zeros((3, ROWS, 256))
    back = np.zeros((ROWS, 768))
    divergence = np.zeros((ROWS, 768))
    squares = np.zeros((ROWS, 256))
    mass_class = pick @ mass
    for m in range(3):
        natural[m, :NAT, :NAT] = parts[m]
        from_class[m, :NAT, :ROWS] = parts[m] @ pick.T
        back[:, ROWS * m : ROWS * m + NAT] = pick @ parts[m].T
        divergence[:, ROWS * m : ROWS * m + NAT] = mass_class[:, None] * (pick @ parts[m])
        squares[:, :NAT] += pick @ (parts[m].astype(np.float32) ** 2).T
    to_natural = np.zeros((ROWS, 256))
    to_natural[:NAT, :ROWS] = pick.T
    mass_natural = np.zeros((ROWS,))
    mass_natural[:NAT] = mass
    pad = (pick.sum(1) == 0).astype(np.float32)
    out = []
    for matrix in (
        natural.reshape(3 * ROWS, 256),
        from_class.reshape(3 * ROWS, 256),
        back,
        divergence,
        squares,
    ):
        out += list(split_np(matrix))
    out.append(to_natural.astype(ml_dtypes.bfloat16))
    wide = lambda v: np.broadcast_to(v[:, None], (ROWS, 128)).astype(np.float32)
    out += [wide(mass_natural), wide(REACTION * mass_class), wide(pad)]
    lane = np.arange(128)[None, :] * np.ones((8, 1), int)
    sub = np.arange(8)[:, None] * np.ones((1, 128), int)
    ex, ey, ez = lane // 64, (lane // 32) % 2, lane % 32
    upper = sub >= 4
    corner_high = (sub % 4) == 2
    corner_low = (sub % 4) == 0
    masks = np.stack(
        [
            ex == 0,
            ex == 1,
            ey == 0,
            ey == 1,
            upper & (ey == 0),
            ~upper & (ey == 1),
            ez < 31,
            ez > 0,
            upper & (ez < 31),
            ~upper & (ez > 0),
            corner_high & (ez < 31),
            corner_low & (ez > 0),
            upper & (ey == 1),
            ~upper & (ey == 0),
            upper & (ey == 1) & (ex == 1),
            ~upper & (ey == 0) & (ex == 1),
            upper & (ey == 1) & (ex == 0),
            ~upper & (ey == 0) & (ex == 0),
        ]
    ).astype(np.float32)
    out.append(masks)
    side_x = [1, 0, 2, 0, 2, 1, 1]
    low_x = np.stack([(s == 0) & (ex == 0) for s in side_x])
    high_x = np.stack([(s == 2) & (ex == 1) for s in side_x])
    none = np.zeros((8, 128), bool)
    low_y = np.stack([none, none, none, ~upper & (ey == 0), ~upper & (ey == 0), ey == 0, none])
    high_y = np.stack([none, none, none, upper & (ey == 1), upper & (ey == 1), none, ey == 1])
    out.append(np.stack([low_x, high_x, low_y, high_y]).astype(np.float32))
    column = np.arange(256)
    place = np.zeros((3, DOM, 256))
    spread = np.zeros((3, 256, 128))
    lanes = np.arange(128)
    for fx in range(3):
        for dom in range(DOM):
            place[fx, dom] = (column // 8) == dom + fx - 1
        f = lanes % 16
        spread[fx] = (
            ((f // 3) == fx)[None, :]
            & (f < 9)[None, :]
            & ((column % 8)[:, None] == (lanes // 16 + f % 3 - 1)[None, :])
        )
    out.append(place.astype(np.float32))
    out.append(spread.reshape(768, 128).astype(ml_dtypes.bfloat16))
    return out


def dot(a, b):
    return jnp.dot(a, b, preferred_element_type=F32)


def halves(x):
    high = x.astype(BF16)
    low = (x - high.astype(F32)).astype(BF16)
    return high, low


def thirds(x):
    high = x.astype(BF16)
    rest = x - high.astype(F32)
    mid = rest.astype(BF16)
    low = (rest - mid.astype(F32)).astype(BF16)
    return high, mid, low


def product(high_ref, low_ref, x):
    depth = high_ref.shape[1]
    if x.shape[0] < depth:
        x = jnp.concatenate([x, jnp.zeros((depth - x.shape[0], x.shape[1]), F32)], axis=0)
    width = x.shape[1]
    high, low = halves(x)
    both = dot(high_ref[...], jnp.concatenate([high, low], axis=1))
    return both[:, :width] + both[:, width:] + dot(low_ref[...], high)


def pad_rows(x, rows):
    return jnp.concatenate([x, jnp.zeros((rows - x.shape[0], x.shape[1]), F32)], axis=0)


def move_lanes(x, select, transposed):
    rows = x.shape[0]
    stacked = jnp.concatenate(thirds(x), axis=0)
    if transposed:
        moved = lax.dot_general(
            stacked, select, (((1,), (1,)), ((), ())), preferred_element_type=F32
        )
    else:
        moved = dot(stacked, select)
    return moved[:rows] + moved[rows : 2 * rows] + moved[2 * rows :]


def roll(x, shift, axis):
    return pltpu.roll(x, shift, axis)


def cube(x):
    return x.reshape(x.shape[0] // 8, 8, 128)


def flat(x):
    return x.reshape(x.shape[0] * 8, 128)


def swap(x):
    return roll(x, 4, 1)


def block_sum(t, mask):
    inner, a0, a5, b0, b5, z0, z5 = (
        t[0:8],
        t[8:13],
        t[13:18],
        t[18:21],
        t[21:24],
        t[24:26],
        t[26:28],
    )
    a0, a5 = a0 + mask(1) * roll(a5, 64, 2), a5 + mask(0) * roll(a0, 64, 2)
    b0, b5 = b0 + mask(3) * roll(b5, 32, 2), b5 + mask(2) * roll(b0, 96, 2)
    edge = jnp.concatenate([a0[3:5], a5[3:5]], axis=0)
    turned = swap(edge)
    edge = edge + mask(4) * roll(turned, 96, 2) + mask(5) * roll(turned, 32, 2)
    z0, z5 = z0 + mask(7) * roll(z5, 1, 2), z5 + mask(6) * roll(z0, 127, 2)
    rim = jnp.concatenate([a0[2:3], a5[2:3], b0[2:3], b5[2:3]], axis=0)
    turned = swap(rim)
    rim = rim + mask(8) * roll(turned, 127, 2) + mask(9) * roll(turned, 1, 2)
    corner = jnp.concatenate([edge[1:2], edge[3:4]], axis=0)
    corner = (
        corner
        + mask(10) * roll(roll(corner, 2, 1), 127, 2)
        + mask(11) * roll(roll(corner, 6, 1), 1, 2)
    )
    return jnp.concatenate(
        [
            inner,
            a0[0:2],
            rim[0:1],
            edge[0:1],
            corner[0:1],
            a5[0:2],
            rim[1:2],
            edge[2:3],
            corner[1:2],
            b0[0:2],
            rim[2:3],
            b5[0:2],
            rim[3:4],
            z0,
            z5,
        ],
        axis=0,
    )


def add_neighbours(t, got, mask, has):
    left, right, down, up = has
    from_right, from_left, from_up, from_down, corners = got
    a0, a5, b0, b5 = t[8:13], t[13:18], t[18:21], t[21:24]
    a5 = a5 + (right * mask(1)) * roll(from_right, 64, 2)
    a0 = a0 + (left * mask(0)) * roll(from_left, 64, 2)
    b5 = b5 + (up * mask(3)) * roll(from_up[0:3], 32, 2)
    b0 = b0 + (down * mask(2)) * roll(from_down[0:3], 96, 2)
    up_rows = (up * mask(12)) * roll(swap(from_up[3:7]), 32, 2)
    down_rows = (down * mask(13)) * roll(swap(from_down[3:7]), 96, 2)
    edge = up_rows + down_rows
    e0 = a0[3:5] + edge[0:2]
    e5 = a5[3:5] + edge[2:4]
    e5 = e5 + (right * up * mask(14)) * roll(swap(corners[0]), 96, 2)
    e5 = e5 + (right * down * mask(15)) * roll(swap(corners[1]), 32, 2)
    e0 = e0 + (left * up * mask(16)) * roll(swap(corners[2]), 96, 2)
    e0 = e0 + (left * down * mask(17)) * roll(swap(corners[3]), 32, 2)
    return jnp.concatenate([t[0:8], a0[0:3], e0, a5[0:3], e5, b0, b5, t[24:28]], axis=0)


def by_kind(t):
    total = lambda *spans: sum(jnp.sum(t[a:b], axis=0, keepdims=True) for a, b in spans)
    return jnp.concatenate(
        [
            total((0, 8), (24, 28)),
            total((8, 11)),
            total((13, 16)),
            total((11, 13)),
            total((16, 18)),
            total((18, 21)),
            total((21, 24)),
        ],
        axis=0,
    )


def from_kinds(v):
    order = [0] * 8 + [1] * 3 + [3] * 2 + [2] * 3 + [4] * 2 + [5] * 3 + [6] * 3 + [0] * 4
    return jnp.concatenate([v[k : k + 1] for k in order], axis=0)


def total_of(x):
    return jnp.sum(jnp.sum(x, axis=0, keepdims=True), axis=2, keepdims=True)


def kernel(
    vel_ref,
    base_ref,
    visc_ref,
    order_ref,
    coarse_ref,
    nat_hi,
    nat_lo,
    cls_hi,
    cls_lo,
    back_hi,
    back_lo,
    div_hi,
    div_lo,
    sq_hi,
    sq_lo,
    out_pick,
    mass_ref,
    react_ref,
    pad_ref,
    mask_ref,
    side_ref,
    place_ref,
    spread_ref,
    lin_ref,
    press_ref,
    field,
    y_up,
    y_down,
    got_x,
    got_y,
    got_c,
    row_a,
    row_b,
    all_a,
    all_b,
    weight_ref,
    solve_ref,
    send_h,
    recv_h,
    send_a,
    recv_a,
    send_b,
    recv_b,
):
    dom = lax.axis_index("dom")
    sub = lax.axis_index("sub")
    dom_next, dom_prev = lax.rem(dom + 1, DOM), lax.rem(dom + DOM - 1, DOM)
    sub_next, sub_prev = lax.rem(sub + 1, SUB), lax.rem(sub + SUB - 1, SUB)
    barrier = pltpu.get_barrier_semaphore()

    def greet(where):
        pl.semaphore_signal(barrier, inc=1, device_id=where, device_id_type=MESH)

    for step in range(1, SUB):
        greet((dom, lax.rem(sub + step, SUB)))
    for step in range(1, DOM):
        greet((lax.rem(dom + step, DOM), sub))
    diagonals = (
        (dom_prev, sub_prev),
        (dom_prev, sub_next),
        (dom_next, sub_prev),
        (dom_next, sub_next),
    )
    for where in diagonals:
        greet(where)

    mask = lambda at: mask_ref[at]

    def flag(condition):
        return jnp.where(condition, 1.0, 0.0).astype(F32)

    has = (flag(dom > 0), flag(dom < DOM - 1), flag(sub > 0), flag(sub < SUB - 1))

    vel = [pad_rows(vel_ref[c], ROWS) for c in range(3)]
    base = [pad_rows(base_ref[c], ROWS) for c in range(3)]
    advect = []
    for c in range(3):
        grads = product(nat_hi, nat_lo, jnp.concatenate([vel[c], base[c]], axis=1))
        acc = jnp.zeros((ROWS, 128), F32)
        for m in range(3):
            part = grads[ROWS * m : ROWS * (m + 1)]
            acc = acc - base[m] * part[:, :128] - vel[m] * part[:, 128:]
        advect.append(acc)
        lin_ref[c] = acc[:NAT]
    select = jnp.where(
        lax.broadcasted_iota(jnp.int32, (128, 128), 0) == order_ref[...], 1.0, 0.0
    ).astype(BF16)
    moved = move_lanes(
        jnp.concatenate(
            [
                product(div_hi, div_lo, jnp.concatenate(advect, axis=0)),
                pad_rows(visc_ref[...], ROWS),
            ],
            axis=0,
        ),
        select,
        True,
    )
    rhs_own = cube(moved[:ROWS])
    weighted = mass_ref[...] * moved[ROWS:]
    weight_ref[...] = jnp.concatenate([weighted, weighted, weighted], axis=0)
    diag_own = cube(react_ref[...] + product(sq_hi, sq_lo, weighted))

    left, right, down, up = has
    side_l, side_r = (0.5 * left) * side_ref[0], (0.5 * right) * side_ref[1]
    side_d, side_u = (0.5 * down) * side_ref[2], (0.5 * up) * side_ref[3]
    along_x = (side_l, 1.0 - side_l - side_r, side_r)
    along_y = (side_d, 1.0 - side_d - side_u, side_u)

    def coarse_parts(kinds):
        return [
            jnp.sum(along_x[fx] * along_y[fy] * kinds, axis=0, keepdims=True)
            for fx in range(3)
            for fy in range(3)
        ]

    def spread_coarse(solved):
        values = 0.0
        for fx in range(3):
            inner = sum(solved[3 * fx + fy] * along_y[fy] for fy in range(3))
            values = values + along_x[fx] * inner
        return from_kinds(values)

    lane = lax.broadcasted_iota(jnp.int32, (16, 128), 1)
    slot = lax.broadcasted_iota(jnp.int32, (16, 128), 0)
    home = lane == 16 * sub + slot

    def send(src, dst, send_sem, recv_sem, where):
        pltpu.make_async_remote_copy(
            src_ref=src,
            dst_ref=dst,
            send_sem=send_sem,
            recv_sem=recv_sem,
            device_id=where,
            device_id_type=MESH,
        ).start()

    def wait_for(ref, sem):
        pltpu.make_async_copy(ref, ref, sem).wait()

    def start_gather(at, partials):
        count = len(partials)
        stack = jnp.concatenate(partials, axis=0)
        sums = jnp.sum(jnp.sum(stack, axis=1), axis=1, keepdims=True)
        if count < 16:
            sums = jnp.concatenate([sums, jnp.zeros((16 - count, 1), F32)], axis=0)
        row = jnp.sum(jnp.where(home, sums, 0.0), axis=0, keepdims=True)
        row_a[at] = row
        for step in range(1, SUB):
            send(
                row_a.at[at],
                all_a.at[at, step - 1],
                send_a.at[at],
                recv_a.at[at],
                (dom, lax.rem(sub + step, SUB)),
            )
        return row

    def forward_gather(at, row):
        wait_for(all_a.at[at], recv_a.at[at])
        row = row + jnp.sum(all_a[at], axis=0)
        row_b[at] = row
        for step in range(1, DOM):
            send(
                row_b.at[at],
                all_b.at[at, dom],
                send_b.at[at],
                recv_b.at[at],
                (lax.rem(dom + step, DOM), sub),
            )
        all_b[at, dom] = row

    def finish_gather(at):
        wait_for(all_b.at[at, 0 : DOM - 1], recv_b.at[at])
        return all_b[at].reshape(DOM, 128)

    def start_halo(at, which, own):
        t = block_sum(own, mask)
        field[at] = t
        y_up[at, 0:3] = t[21:24]
        y_up[at, 3:5] = t[11:13]
        y_up[at, 5:7] = t[16:18]
        y_down[at, 0:3] = t[18:21]
        y_down[at, 3:5] = t[11:13]
        y_down[at, 5:7] = t[16:18]
        ss, rs = send_h.at[which], recv_h.at[which]
        send(field.at[at, 8:13], got_x.at[at, 0], ss.at[0], rs.at[0], (dom_prev, sub))
        send(field.at[at, 13:18], got_x.at[at, 1], ss.at[0], rs.at[0], (dom_next, sub))
        send(y_down.at[at], got_y.at[at, 0], ss.at[1], rs.at[1], (dom, sub_prev))
        send(y_up.at[at], got_y.at[at, 1], ss.at[1], rs.at[1], (dom, sub_next))
        for n, where in enumerate(diagonals):
            src = field.at[at, 11:13] if n < 2 else field.at[at, 16:18]
            send(src, got_c.at[at, n], ss.at[2], rs.at[2], where)
        return t

    def finish_halo(at, which, t):
        rs = recv_h.at[which]
        wait_for(got_x.at[at], rs.at[0])
        wait_for(got_y.at[at], rs.at[1])
        wait_for(got_c.at[at], rs.at[2])
        got = (
            got_x[at, 0],
            got_x[at, 1],
            got_y[at, 0],
            got_y[at, 1],
            [got_c[at, n] for n in range(4)],
        )
        return add_neighbours(t, got, mask, has)

    def apply(u):
        v = flat(u)
        g = product(cls_hi, cls_lo, v)
        h = pad_rows(g * weight_ref[...], 768)
        return cube(product(back_hi, back_lo, h) + react_ref[...] * v)

    def inner(a, b):
        return jnp.sum(a * b, axis=0, keepdims=True)

    def results(everyone, dots):
        rows = cube(everyone)
        terms = [
            jnp.sum(rows * cube(solve_ref[a]), axis=0, keepdims=True) for a in range(NFACE)
        ]
        column = jnp.sum(rows, axis=0, keepdims=True)
        which = lax.broadcasted_iota(jnp.int32, (1, 8, 128), 2) % 16
        terms += [jnp.where(which == NFACE + d, column, 0.0) for d in range(dots)]
        sums = jnp.sum(
            jnp.sum(jnp.concatenate(terms, axis=0), axis=1, keepdims=True), axis=2, keepdims=True
        )
        return [sums[n] for n in range(NFACE + dots)]

    pl.semaphore_wait(barrier, SUB - 1 + DOM - 1 + 4)
    row = start_gather(0, coarse_parts(by_kind(rhs_own)))
    rhs_block = start_halo(0, 0, rhs_own)
    diag_block = start_halo(1, 1, diag_own)

    chosen = []
    for ax in (-1, 0, 1):
        for ay in (-1, 0, 1):
            at = jnp.clip((dom + ax) * SUB + sub + ay, 0, DOM * SUB - 1)
            chosen.append(coarse_ref[pl.ds(at, 1), :])
    for a in range(NFACE):
        wide = jnp.concatenate([place_ref[fx] * chosen[a] for fx in range(3)], axis=1)
        pieces = thirds(wide)
        solve_ref[a] = sum(dot(piece, spread_ref[...]) for piece in pieces)

    forward_gather(0, row)
    r_all = finish_halo(0, 0, rhs_block)
    d_all = finish_halo(1, 1, diag_block)
    inverse = 1.0 / (d_all + cube(pad_ref[...]))
    solved = results(finish_gather(0), 0)
    r_own = rhs_own
    z = inverse * r_all + spread_coarse(solved)

    direction = None
    for it in range(3):
        w_own = apply(z)
        dots = [inner(z, r_own), inner(z, w_own)]
        last = it == 2
        parts = coarse_parts(by_kind(w_own)) if not last else [jnp.zeros((1, 8, 128), F32)] * 9
        row = start_gather(it + 1, parts + dots)
        if not last:
            w_block = start_halo(it + 2, it + 2, w_own)
        forward_gather(it + 1, row)
        if not last:
            w_all = finish_halo(it + 2, it + 2, w_block)
        got = results(finish_gather(it + 1), 2)
        gamma, curve = got[NFACE], got[NFACE + 1]
        solved_w = got[:NFACE]
        if it == 0:
            alpha = gamma / curve
            direction = z
            q = alpha * direction
            if not last:
                along_own, along_all, along_solved = w_own, w_all, solved_w
        else:
            beta = gamma / gamma_before
            alpha = gamma / (curve - beta * gamma / alpha)
            direction = z + beta * direction
            q = q + alpha * direction
            if not last:
                along_own = w_own + beta * along_own
                along_all = w_all + beta * along_all
                along_solved = [a + beta * b for a, b in zip(solved_w, along_solved)]
        gamma_before = gamma
        if not last:
            r_own = r_own - alpha * along_own
            r_all = r_all - alpha * along_all
            solved = [a - alpha * b for a, b in zip(solved, along_solved)]
            z = inverse * r_all + spread_coarse(solved)

    slots = pad_rows(move_lanes(flat(q), select, False), 256)
    press_ref[...] = sum(dot(out_pick[...], piece) for piece in thirds(slots))[:NAT]
    grads = product(cls_hi, cls_lo, slots)
    for c in range(3):
        lin_ref[c] = lin_ref[c] - grads[ROWS * c : ROWS * c + NAT]

    for at in range(4):
        wait_for(all_a.at[at], send_a.at[at])
        wait_for(all_b.at[at, 0 : DOM - 1], send_b.at[at])
        wait_for(got_x.at[at], send_h.at[at, 0])
        wait_for(got_y.at[at], send_h.at[at, 1])
        wait_for(got_c.at[at], send_h.at[at, 2])


def shards(velocity, base_flow, viscosity, cell_order, coarse_inv):
    args = [velocity, base_flow, viscosity, cell_order, coarse_inv]
    args += [jnp.asarray(t) for t in tables()]
    vmem = pl.BlockSpec(memory_space=pltpu.VMEM)
    dma = pltpu.SemaphoreType.DMA
    return pl.pallas_call(
        kernel,
        out_shape=(
            jax.ShapeDtypeStruct((3, NAT, 128), F32),
            jax.ShapeDtypeStruct((NAT, 128), F32),
        ),
        in_specs=[vmem] * len(args),
        out_specs=(vmem, vmem),
        scratch_shapes=[
            pltpu.VMEM((4, 28, 8, 128), F32),
            pltpu.VMEM((4, 7, 8, 128), F32),
            pltpu.VMEM((4, 7, 8, 128), F32),
            pltpu.VMEM((4, 2, 5, 8, 128), F32),
            pltpu.VMEM((4, 2, 7, 8, 128), F32),
            pltpu.VMEM((4, 4, 2, 8, 128), F32),
            pltpu.VMEM((4, 1, 128), F32),
            pltpu.VMEM((4, 1, 128), F32),
            pltpu.VMEM((4, SUB - 1, 1, 128), F32),
            pltpu.VMEM((4, DOM, 1, 128), F32),
            pltpu.VMEM((3 * ROWS, 128), F32),
            pltpu.VMEM((NFACE, DOM, 128), F32),
            dma((4, 3)),
            dma((4, 3)),
            dma((4,)),
            dma((4,)),
            dma((4,)),
            dma((4,)),
        ],
        compiler_params=pltpu.CompilerParams(
            collective_id=0, has_side_effects=True, vmem_limit_bytes=48 << 20
        ),
    )(*args)


def solution(mesh):
    placed = (
        P(None, None, ("dom", "sub")),
        P(None, None, ("dom", "sub")),
        P(None, ("dom", "sub")),
        P(("dom", "sub"), None),
        P(),
    )
    return jax.shard_map(
        shards,
        mesh=mesh,
        in_specs=placed,
        out_specs=(P(None, None, ("dom", "sub")), P(None, ("dom", "sub"))),
        check_vma=False,
    )
```

```python
import functools

import jax
import jax.numpy as jnp
import ml_dtypes
import numpy as np
from jax import lax
from jax.experimental import pallas as pl
from jax.experimental.pallas import tpu as pltpu
from jax.sharding import PartitionSpec as P

F32 = jnp.float32
BF16 = jnp.bfloat16
MESH = pl.DeviceIdType.MESH
REACTION = 0.001
DOM = 32
SUB = 8
ROWS = 224
NAT = 216
NFACE = 9


def gll_tables():
    points = np.array(
        [
            -1.0,
            -0.7650553239294647,
            -0.2852315164806451,
            0.2852315164806451,
            0.7650553239294647,
            1.0,
        ]
    )
    weights = np.array(
        [
            1.0 / 15.0,
            0.378474956297847,
            0.5548583770354862,
            0.5548583770354862,
            0.378474956297847,
            1.0 / 15.0,
        ]
    )
    legendre = (63.0 * points**5 - 70.0 * points**3 + 15.0 * points) / 8.0
    derivative = np.zeros((6, 6))
    for a in range(6):
        for b in range(6):
            if a != b:
                derivative[a, b] = legendre[a] / (legendre[b] * (points[a] - points[b]))
    derivative[0, 0] = -7.5
    derivative[5, 5] = 7.5
    mass = weights[:, None, None] * weights[None, :, None] * weights[None, None, :]
    return (
        derivative.astype(np.float32).astype(np.float64),
        mass.astype(np.float32).astype(np.float64).reshape(-1),
    )


def class_rows():
    mid = (1, 2, 3, 4)
    rows = [(i, j, k) for i in mid for j in mid for k in mid]
    for i in (0, 5):
        rows += [(i, j, k) for j in mid for k in mid]
        rows += [(i, j, k) for k in (0, 5) for j in mid]
        rows += [(i, j, k) for j in (0, 5) for k in mid]
        for j in (0, 5):
            for k in (0, 5):
                rows += [(i, j, k), None]
    for j in (0, 5):
        rows += [(i, j, k) for i in mid for k in mid]
        rows += [(i, j, k) for k in (0, 5) for i in mid]
    for k in (0, 5):
        rows += [(i, j, k) for i in mid for j in mid]
    return rows


def split_np(matrix):
    single = matrix.astype(np.float32)
    high = single.astype(ml_dtypes.bfloat16)
    low = (single - high.astype(np.float32)).astype(ml_dtypes.bfloat16)
    return high, low


def tables():
    derivative, mass = gll_tables()
    eye = np.eye(6)
    parts = [
        np.kron(np.kron(derivative, eye), eye),
        np.kron(np.kron(eye, derivative), eye),
        np.kron(np.kron(eye, eye), derivative),
    ]
    rows = class_rows()
    assert len(rows) == ROWS
    pick = np.zeros((ROWS, NAT))
    for at, node in enumerate(rows):
        if node is not None:
            pick[at, 36 * node[0] + 6 * node[1] + node[2]] = 1.0
    natural = np.zeros((3, ROWS, 256))
    from_class = np.zeros((3, ROWS, 256))
    back = np.zeros((ROWS, 768))
    divergence = np.zeros((ROWS, 768))
    squares = np.zeros((ROWS, 256))
    mass_class = pick @ mass
    for m in range(3):
        natural[m, :NAT, :NAT] = parts[m]
        from_class[m, :NAT, :ROWS] = parts[m] @ pick.T
        back[:, ROWS * m : ROWS * m + NAT] = pick @ parts[m].T
        divergence[:, ROWS * m : ROWS * m + NAT] = mass_class[:, None] * (pick @ parts[m])
        squares[:, :NAT] += pick @ (parts[m].astype(np.float32) ** 2).T
    to_natural = np.zeros((ROWS, 256))
    to_natural[:NAT, :ROWS] = pick.T
    mass_natural = np.zeros((ROWS,))
    mass_natural[:NAT] = mass
    pad = (pick.sum(1) == 0).astype(np.float32)
    out = []
    for matrix in (
        natural.reshape(3 * ROWS, 256),
        from_class.reshape(3 * ROWS, 256),
        back,
        divergence,
        squares,
    ):
        out += list(split_np(matrix))
    out.append(to_natural.astype(ml_dtypes.bfloat16))
    wide = lambda v: np.broadcast_to(v[:, None], (ROWS, 128)).astype(np.float32)
    out += [wide(mass_natural), wide(REACTION * mass_class), wide(pad)]
    lane = np.arange(128)[None, :] * np.ones((8, 1), int)
    sub = np.arange(8)[:, None] * np.ones((1, 128), int)
    ex, ey, ez = lane // 64, (lane // 32) % 2, lane % 32
    upper = sub >= 4
    corner_high = (sub % 4) == 2
    corner_low = (sub % 4) == 0
    masks = np.stack(
        [
            ex == 0,
            ex == 1,
            ey == 0,
            ey == 1,
            upper & (ey == 0),
            ~upper & (ey == 1),
            ez < 31,
            ez > 0,
            upper & (ez < 31),
            ~upper & (ez > 0),
            corner_high & (ez < 31),
            corner_low & (ez > 0),
            upper & (ey == 1),
            ~upper & (ey == 0),
            upper & (ey == 1) & (ex == 1),
            ~upper & (ey == 0) & (ex == 1),
            upper & (ey == 1) & (ex == 0),
            ~upper & (ey == 0) & (ex == 0),
        ]
    ).astype(np.float32)
    out.append(masks)
    side_x = [1, 0, 2, 0, 2, 1, 1]
    low_x = np.stack([(s == 0) & (ex == 0) for s in side_x])
    high_x = np.stack([(s == 2) & (ex == 1) for s in side_x])
    none = np.zeros((8, 128), bool)
    low_y = np.stack([none, none, none, ~upper & (ey == 0), ~upper & (ey == 0), ey == 0, none])
    high_y = np.stack([none, none, none, upper & (ey == 1), upper & (ey == 1), none, ey == 1])
    out.append(np.stack([low_x, high_x, low_y, high_y]).astype(np.float32))
    column = np.arange(256)
    place = np.zeros((3, DOM, 256))
    spread = np.zeros((3, 256, 128))
    lanes = np.arange(128)
    for fx in range(3):
        for dom in range(DOM):
            place[fx, dom] = (column // 8) == dom + fx - 1
        f = lanes % 16
        spread[fx] = (
            ((f // 3) == fx)[None, :]
            & (f < 9)[None, :]
            & ((column % 8)[:, None] == (lanes // 16 + f % 3 - 1)[None, :])
        )
    out.append(place.astype(np.float32))
    out.append(spread.reshape(768, 128).astype(ml_dtypes.bfloat16))
    return out


def dot(a, b):
    return jnp.dot(a, b, preferred_element_type=F32)


def halves(x):
    high = x.astype(BF16)
    low = (x - high.astype(F32)).astype(BF16)
    return high, low


def thirds(x):
    high = x.astype(BF16)
    rest = x - high.astype(F32)
    mid = rest.astype(BF16)
    low = (rest - mid.astype(F32)).astype(BF16)
    return high, mid, low


def product(high_ref, low_ref, x):
    depth = high_ref.shape[1]
    if x.shape[0] < depth:
        x = jnp.concatenate([x, jnp.zeros((depth - x.shape[0], x.shape[1]), F32)], axis=0)
    width = x.shape[1]
    high, low = halves(x)
    both = dot(high_ref[...], jnp.concatenate([high, low], axis=1))
    return both[:, :width] + both[:, width:] + dot(low_ref[...], high)


def pad_rows(x, rows):
    return jnp.concatenate([x, jnp.zeros((rows - x.shape[0], x.shape[1]), F32)], axis=0)


def move_lanes(x, select, transposed):
    rows = x.shape[0]
    stacked = jnp.concatenate(thirds(x), axis=0)
    if transposed:
        moved = lax.dot_general(
            stacked, select, (((1,), (1,)), ((), ())), preferred_element_type=F32
        )
    else:
        moved = dot(stacked, select)
    return moved[:rows] + moved[rows : 2 * rows] + moved[2 * rows :]


def roll(x, shift, axis):
    return pltpu.roll(x, shift, axis)


def cube(x):
    return x.reshape(x.shape[0] // 8, 8, 128)


def flat(x):
    return x.reshape(x.shape[0] * 8, 128)


def swap(x):
    return roll(x, 4, 1)


def block_sum(t, mask):
    inner, a0, a5, b0, b5, z0, z5 = (
        t[0:8],
        t[8:13],
        t[13:18],
        t[18:21],
        t[21:24],
        t[24:26],
        t[26:28],
    )
    a0, a5 = a0 + mask(1) * roll(a5, 64, 2), a5 + mask(0) * roll(a0, 64, 2)
    b0, b5 = b0 + mask(3) * roll(b5, 32, 2), b5 + mask(2) * roll(b0, 96, 2)
    edge = jnp.concatenate([a0[3:5], a5[3:5]], axis=0)
    turned = swap(edge)
    edge = edge + mask(4) * roll(turned, 96, 2) + mask(5) * roll(turned, 32, 2)
    z0, z5 = z0 + mask(7) * roll(z5, 1, 2), z5 + mask(6) * roll(z0, 127, 2)
    rim = jnp.concatenate([a0[2:3], a5[2:3], b0[2:3], b5[2:3]], axis=0)
    turned = swap(rim)
    rim = rim + mask(8) * roll(turned, 127, 2) + mask(9) * roll(turned, 1, 2)
    corner = jnp.concatenate([edge[1:2], edge[3:4]], axis=0)
    corner = (
        corner
        + mask(10) * roll(roll(corner, 2, 1), 127, 2)
        + mask(11) * roll(roll(corner, 6, 1), 1, 2)
    )
    return jnp.concatenate(
        [
            inner,
            a0[0:2],
            rim[0:1],
            edge[0:1],
            corner[0:1],
            a5[0:2],
            rim[1:2],
            edge[2:3],
            corner[1:2],
            b0[0:2],
            rim[2:3],
            b5[0:2],
            rim[3:4],
            z0,
            z5,
        ],
        axis=0,
    )


def add_neighbours(t, got, mask, has):
    left, right, down, up = has
    from_right, from_left, from_up, from_down, corners = got
    a0, a5, b0, b5 = t[8:13], t[13:18], t[18:21], t[21:24]
    a5 = a5 + (right * mask(1)) * roll(from_right, 64, 2)
    a0 = a0 + (left * mask(0)) * roll(from_left, 64, 2)
    b5 = b5 + (up * mask(3)) * roll(from_up[0:3], 32, 2)
    b0 = b0 + (down * mask(2)) * roll(from_down[0:3], 96, 2)
    up_rows = (up * mask(12)) * roll(swap(from_up[3:7]), 32, 2)
    down_rows = (down * mask(13)) * roll(swap(from_down[3:7]), 96, 2)
    edge = up_rows + down_rows
    e0 = a0[3:5] + edge[0:2]
    e5 = a5[3:5] + edge[2:4]
    e5 = e5 + (right * up * mask(14)) * roll(swap(corners[0]), 96, 2)
    e5 = e5 + (right * down * mask(15)) * roll(swap(corners[1]), 32, 2)
    e0 = e0 + (left * up * mask(16)) * roll(swap(corners[2]), 96, 2)
    e0 = e0 + (left * down * mask(17)) * roll(swap(corners[3]), 32, 2)
    return jnp.concatenate([t[0:8], a0[0:3], e0, a5[0:3], e5, b0, b5, t[24:28]], axis=0)


def by_kind(t):
    total = lambda *spans: sum(jnp.sum(t[a:b], axis=0, keepdims=True) for a, b in spans)
    return jnp.concatenate(
        [
            total((0, 8), (24, 28)),
            total((8, 11)),
            total((13, 16)),
            total((11, 13)),
            total((16, 18)),
            total((18, 21)),
            total((21, 24)),
        ],
        axis=0,
    )


def from_kinds(v):
    order = [0] * 8 + [1] * 3 + [3] * 2 + [2] * 3 + [4] * 2 + [5] * 3 + [6] * 3 + [0] * 4
    return jnp.concatenate([v[k : k + 1] for k in order], axis=0)


def total_of(x):
    return jnp.sum(jnp.sum(x, axis=0, keepdims=True), axis=2, keepdims=True)


NAMES = (
    "vel",
    "base",
    "visc",
    "order",
    "coarse",
    "nat_hi",
    "nat_lo",
    "cls_hi",
    "cls_lo",
    "back_hi",
    "back_lo",
    "div_hi",
    "div_lo",
    "sq_hi",
    "sq_lo",
    "out_pick",
    "mass",
    "react",
    "pad",
    "mask",
    "side",
    "place",
    "spread",
)
ORDER = (
    "nat_hi",
    "vel",
    "base",
    "nat_lo",
    "div_hi",
    "div_lo",
    "order",
    "visc",
    "mask",
    "side",
    "mass",
    "sq_hi",
    "sq_lo",
    "react",
    "coarse",
    "place",
    "spread",
    "pad",
    "cls_hi",
    "cls_lo",
    "back_hi",
    "back_lo",
    "out_pick",
)


def kernel(*refs):
    count = len(NAMES)
    sources = dict(zip(NAMES, refs[:count]))
    lin_ref, press_ref = refs[count : count + 2]
    held = dict(zip(NAMES, refs[count + 2 : 2 * count + 2]))
    (
        load_sem,
        field,
        y_up,
        y_down,
        got_x,
        got_y,
        got_c,
        row_a,
        row_b,
        all_a,
        all_b,
        weight_ref,
        solve_ref,
        send_h,
        recv_h,
        send_a,
        recv_a,
        send_b,
        recv_b,
    ) = refs[2 * count + 2 :]
    loads = {
        name: pltpu.make_async_copy(sources[name], held[name], load_sem.at[at])
        for at, name in enumerate(NAMES)
    }
    for name in ORDER:
        loads[name].start()
    ready = set()

    def need(name):
        if name not in ready:
            loads[name].wait()
            ready.add(name)
        return held[name]

    dom = lax.axis_index("dom")
    sub = lax.axis_index("sub")
    dom_next, dom_prev = lax.rem(dom + 1, DOM), lax.rem(dom + DOM - 1, DOM)
    sub_next, sub_prev = lax.rem(sub + 1, SUB), lax.rem(sub + SUB - 1, SUB)
    barrier = pltpu.get_barrier_semaphore()

    def greet(where):
        pl.semaphore_signal(barrier, inc=1, device_id=where, device_id_type=MESH)

    for step in range(1, SUB):
        greet((dom, lax.rem(sub + step, SUB)))
    for step in range(1, DOM):
        greet((lax.rem(dom + step, DOM), sub))
    diagonals = (
        (dom_prev, sub_prev),
        (dom_prev, sub_next),
        (dom_next, sub_prev),
        (dom_next, sub_next),
    )
    for where in diagonals:
        greet(where)

    mask = lambda at: need("mask")[at]

    def flag(condition):
        return jnp.where(condition, 1.0, 0.0).astype(F32)

    has = (flag(dom > 0), flag(dom < DOM - 1), flag(sub > 0), flag(sub < SUB - 1))

    vel = [pad_rows(need("vel")[c], ROWS) for c in range(3)]
    base = [pad_rows(need("base")[c], ROWS) for c in range(3)]
    advect = []
    for c in range(3):
        grads = product(need("nat_hi"), need("nat_lo"), jnp.concatenate([vel[c], base[c]], axis=1))
        acc = jnp.zeros((ROWS, 128), F32)
        for m in range(3):
            part = grads[ROWS * m : ROWS * (m + 1)]
            acc = acc - base[m] * part[:, :128] - vel[m] * part[:, 128:]
        advect.append(acc)
        lin_ref[c] = acc[:NAT]
    select = jnp.where(
        lax.broadcasted_iota(jnp.int32, (128, 128), 0) == need("order")[...], 1.0, 0.0
    ).astype(BF16)
    moved = move_lanes(
        jnp.concatenate(
            [
                product(need("div_hi"), need("div_lo"), jnp.concatenate(advect, axis=0)),
                pad_rows(need("visc")[...], ROWS),
            ],
            axis=0,
        ),
        select,
        True,
    )
    rhs_own = cube(moved[:ROWS])
    weighted = need("mass")[...] * moved[ROWS:]
    weight_ref[...] = jnp.concatenate([weighted, weighted, weighted], axis=0)
    diag_own = cube(need("react")[...] + product(need("sq_hi"), need("sq_lo"), weighted))

    left, right, down, up = has
    side_l, side_r = (0.5 * left) * need("side")[0], (0.5 * right) * need("side")[1]
    side_d, side_u = (0.5 * down) * need("side")[2], (0.5 * up) * need("side")[3]
    along_x = (side_l, 1.0 - side_l - side_r, side_r)
    along_y = (side_d, 1.0 - side_d - side_u, side_u)

    def coarse_parts(kinds):
        return [
            jnp.sum(along_x[fx] * along_y[fy] * kinds, axis=0, keepdims=True)
            for fx in range(3)
            for fy in range(3)
        ]

    def spread_coarse(solved):
        values = 0.0
        for fx in range(3):
            inner = sum(solved[3 * fx + fy] * along_y[fy] for fy in range(3))
            values = values + along_x[fx] * inner
        return from_kinds(values)

    lane = lax.broadcasted_iota(jnp.int32, (16, 128), 1)
    slot = lax.broadcasted_iota(jnp.int32, (16, 128), 0)
    home = lane == 16 * sub + slot

    def send(src, dst, send_sem, recv_sem, where):
        pltpu.make_async_remote_copy(
            src_ref=src,
            dst_ref=dst,
            send_sem=send_sem,
            recv_sem=recv_sem,
            device_id=where,
            device_id_type=MESH,
        ).start()

    def wait_for(ref, sem):
        pltpu.make_async_copy(ref, ref, sem).wait()

    def start_gather(at, partials):
        count = len(partials)
        stack = jnp.concatenate(partials, axis=0)
        sums = jnp.sum(jnp.sum(stack, axis=1), axis=1, keepdims=True)
        if count < 16:
            sums = jnp.concatenate([sums, jnp.zeros((16 - count, 1), F32)], axis=0)
        row = jnp.sum(jnp.where(home, sums, 0.0), axis=0, keepdims=True)
        row_a[at] = row
        for step in range(1, SUB):
            send(
                row_a.at[at],
                all_a.at[at, step - 1],
                send_a.at[at],
                recv_a.at[at],
                (dom, lax.rem(sub + step, SUB)),
            )
        return row

    def forward_gather(at, row):
        wait_for(all_a.at[at], recv_a.at[at])
        row = row + jnp.sum(all_a[at], axis=0)
        row_b[at] = row
        for step in range(1, DOM):
            send(
                row_b.at[at],
                all_b.at[at, dom],
                send_b.at[at],
                recv_b.at[at],
                (lax.rem(dom + step, DOM), sub),
            )
        all_b[at, dom] = row

    def finish_gather(at):
        wait_for(all_b.at[at, 0 : DOM - 1], recv_b.at[at])
        return all_b[at].reshape(DOM, 128)

    def start_halo(at, which, own):
        t = block_sum(own, mask)
        field[at] = t
        y_up[at, 0:3] = t[21:24]
        y_up[at, 3:5] = t[11:13]
        y_up[at, 5:7] = t[16:18]
        y_down[at, 0:3] = t[18:21]
        y_down[at, 3:5] = t[11:13]
        y_down[at, 5:7] = t[16:18]
        ss, rs = send_h.at[which], recv_h.at[which]
        send(field.at[at, 8:13], got_x.at[at, 0], ss.at[0], rs.at[0], (dom_prev, sub))
        send(field.at[at, 13:18], got_x.at[at, 1], ss.at[0], rs.at[0], (dom_next, sub))
        send(y_down.at[at], got_y.at[at, 0], ss.at[1], rs.at[1], (dom, sub_prev))
        send(y_up.at[at], got_y.at[at, 1], ss.at[1], rs.at[1], (dom, sub_next))
        for n, where in enumerate(diagonals):
            src = field.at[at, 11:13] if n < 2 else field.at[at, 16:18]
            send(src, got_c.at[at, n], ss.at[2], rs.at[2], where)
        return t

    def finish_halo(at, which, t):
        rs = recv_h.at[which]
        wait_for(got_x.at[at], rs.at[0])
        wait_for(got_y.at[at], rs.at[1])
        wait_for(got_c.at[at], rs.at[2])
        got = (
            got_x[at, 0],
            got_x[at, 1],
            got_y[at, 0],
            got_y[at, 1],
            [got_c[at, n] for n in range(4)],
        )
        return add_neighbours(t, got, mask, has)

    def apply(u):
        v = flat(u)
        g = product(need("cls_hi"), need("cls_lo"), v)
        h = pad_rows(g * weight_ref[...], 768)
        return cube(product(need("back_hi"), need("back_lo"), h) + need("react")[...] * v)

    def inner(a, b):
        return jnp.sum(a * b, axis=0, keepdims=True)

    def results(everyone, dots):
        rows = cube(everyone)
        terms = [
            jnp.sum(rows * cube(solve_ref[a]), axis=0, keepdims=True) for a in range(NFACE)
        ]
        column = jnp.sum(rows, axis=0, keepdims=True)
        which = lax.broadcasted_iota(jnp.int32, (1, 8, 128), 2) % 16
        terms += [jnp.where(which == NFACE + d, column, 0.0) for d in range(dots)]
        sums = jnp.sum(
            jnp.sum(jnp.concatenate(terms, axis=0), axis=1, keepdims=True), axis=2, keepdims=True
        )
        return [sums[n] for n in range(NFACE + dots)]

    pl.semaphore_wait(barrier, SUB - 1 + DOM - 1 + 4)
    row = start_gather(0, coarse_parts(by_kind(rhs_own)))
    rhs_block = start_halo(0, 0, rhs_own)
    diag_block = start_halo(1, 1, diag_own)

    chosen = []
    for ax in (-1, 0, 1):
        for ay in (-1, 0, 1):
            at = jnp.clip((dom + ax) * SUB + sub + ay, 0, DOM * SUB - 1)
            chosen.append(need("coarse")[pl.ds(at, 1), :])
    for a in range(NFACE):
        wide = jnp.concatenate([need("place")[fx] * chosen[a] for fx in range(3)], axis=1)
        pieces = thirds(wide)
        solve_ref[a] = sum(dot(piece, need("spread")[...]) for piece in pieces)

    forward_gather(0, row)
    r_all = finish_halo(0, 0, rhs_block)
    d_all = finish_halo(1, 1, diag_block)
    inverse = 1.0 / (d_all + cube(need("pad")[...]))
    solved = results(finish_gather(0), 0)
    r_own = rhs_own
    z = inverse * r_all + spread_coarse(solved)

    direction = None
    for it in range(3):
        w_own = apply(z)
        dots = [inner(z, r_own), inner(z, w_own)]
        last = it == 2
        parts = coarse_parts(by_kind(w_own)) if not last else [jnp.zeros((1, 8, 128), F32)] * 9
        row = start_gather(it + 1, parts + dots)
        if not last:
            w_block = start_halo(it + 2, it + 2, w_own)
        forward_gather(it + 1, row)
        if not last:
            w_all = finish_halo(it + 2, it + 2, w_block)
        got = results(finish_gather(it + 1), 2)
        gamma, curve = got[NFACE], got[NFACE + 1]
        solved_w = got[:NFACE]
        if it == 0:
            alpha = gamma / curve
            direction = z
            q = alpha * direction
            if not last:
                along_own, along_all, along_solved = w_own, w_all, solved_w
        else:
            beta = gamma / gamma_before
            alpha = gamma / (curve - beta * gamma / alpha)
            direction = z + beta * direction
            q = q + alpha * direction
            if not last:
                along_own = w_own + beta * along_own
                along_all = w_all + beta * along_all
                along_solved = [a + beta * b for a, b in zip(solved_w, along_solved)]
        gamma_before = gamma
        if not last:
            r_own = r_own - alpha * along_own
            r_all = r_all - alpha * along_all
            solved = [a - alpha * b for a, b in zip(solved, along_solved)]
            z = inverse * r_all + spread_coarse(solved)

    slots = pad_rows(move_lanes(flat(q), select, False), 256)
    press_ref[...] = sum(dot(need("out_pick")[...], piece) for piece in thirds(slots))[:NAT]
    grads = product(need("cls_hi"), need("cls_lo"), slots)
    for c in range(3):
        lin_ref[c] = lin_ref[c] - grads[ROWS * c : ROWS * c + NAT]

    for at in range(4):
        wait_for(all_a.at[at], send_a.at[at])
        wait_for(all_b.at[at, 0 : DOM - 1], send_b.at[at])
        wait_for(got_x.at[at], send_h.at[at, 0])
        wait_for(got_y.at[at], send_h.at[at, 1])
        wait_for(got_c.at[at], send_h.at[at, 2])


def shards(velocity, base_flow, viscosity, cell_order, coarse_inv):
    args = [velocity, base_flow, viscosity, cell_order, coarse_inv]
    args += [jnp.asarray(t) for t in tables()]
    vmem = pl.BlockSpec(memory_space=pltpu.VMEM)
    hbm = pl.BlockSpec(memory_space=pltpu.HBM)
    dma = pltpu.SemaphoreType.DMA
    return pl.pallas_call(
        kernel,
        out_shape=(
            jax.ShapeDtypeStruct((3, NAT, 128), F32),
            jax.ShapeDtypeStruct((NAT, 128), F32),
        ),
        in_specs=[hbm] * len(args),
        out_specs=(vmem, vmem),
        scratch_shapes=[pltpu.VMEM(arg.shape, arg.dtype) for arg in args]
        + [
            dma((len(args),)),
            pltpu.VMEM((4, 28, 8, 128), F32),
            pltpu.VMEM((4, 7, 8, 128), F32),
            pltpu.VMEM((4, 7, 8, 128), F32),
            pltpu.VMEM((4, 2, 5, 8, 128), F32),
            pltpu.VMEM((4, 2, 7, 8, 128), F32),
            pltpu.VMEM((4, 4, 2, 8, 128), F32),
            pltpu.VMEM((4, 1, 128), F32),
            pltpu.VMEM((4, 1, 128), F32),
            pltpu.VMEM((4, SUB - 1, 1, 128), F32),
            pltpu.VMEM((4, DOM, 1, 128), F32),
            pltpu.VMEM((3 * ROWS, 128), F32),
            pltpu.VMEM((NFACE, DOM, 128), F32),
            dma((4, 3)),
            dma((4, 3)),
            dma((4,)),
            dma((4,)),
            dma((4,)),
            dma((4,)),
        ],
        compiler_params=pltpu.CompilerParams(
            collective_id=0, has_side_effects=True, vmem_limit_bytes=62 << 20
        ),
    )(*args)


def solution(mesh):
    placed = (
        P(None, None, ("dom", "sub")),
        P(None, None, ("dom", "sub")),
        P(None, ("dom", "sub")),
        P(("dom", "sub"), None),
        P(),
    )
    return jax.shard_map(
        shards,
        mesh=mesh,
        in_specs=placed,
        out_specs=(P(None, None, ("dom", "sub")), P(None, ("dom", "sub"))),
        check_vma=False,
    )
```

```python
import functools

import jax
import jax.numpy as jnp
import ml_dtypes
import numpy as np
from jax import lax
from jax.experimental import pallas as pl
from jax.experimental.pallas import tpu as pltpu
from jax.sharding import PartitionSpec as P

F32 = jnp.float32
BF16 = jnp.bfloat16
MESH = pl.DeviceIdType.MESH
REACTION = 0.001
DOM = 32
SUB = 8
CHIPS = 128
ROWS = 224
NAT = 216
NFACE = 9


def gll_tables():
    points = np.array(
        [
            -1.0,
            -0.7650553239294647,
            -0.2852315164806451,
            0.2852315164806451,
            0.7650553239294647,
            1.0,
        ]
    )
    weights = np.array(
        [
            1.0 / 15.0,
            0.378474956297847,
            0.5548583770354862,
            0.5548583770354862,
            0.378474956297847,
            1.0 / 15.0,
        ]
    )
    legendre = (63.0 * points**5 - 70.0 * points**3 + 15.0 * points) / 8.0
    derivative = np.zeros((6, 6))
    for a in range(6):
        for b in range(6):
            if a != b:
                derivative[a, b] = legendre[a] / (legendre[b] * (points[a] - points[b]))
    derivative[0, 0] = -7.5
    derivative[5, 5] = 7.5
    mass = weights[:, None, None] * weights[None, :, None] * weights[None, None, :]
    return (
        derivative.astype(np.float32).astype(np.float64),
        mass.astype(np.float32).astype(np.float64).reshape(-1),
    )


def class_rows():
    mid = (1, 2, 3, 4)
    rows = [(i, j, k) for i in mid for j in mid for k in mid]
    for i in (0, 5):
        rows += [(i, j, k) for j in mid for k in mid]
        rows += [(i, j, k) for k in (0, 5) for j in mid]
        rows += [(i, j, k) for j in (0, 5) for k in mid]
        for j in (0, 5):
            for k in (0, 5):
                rows += [(i, j, k), None]
    for j in (0, 5):
        rows += [(i, j, k) for i in mid for k in mid]
        rows += [(i, j, k) for k in (0, 5) for i in mid]
    for k in (0, 5):
        rows += [(i, j, k) for i in mid for j in mid]
    return rows


def split_np(matrix):
    single = matrix.astype(np.float32)
    high = single.astype(ml_dtypes.bfloat16)
    low = (single - high.astype(np.float32)).astype(ml_dtypes.bfloat16)
    return high, low


def tables():
    derivative, mass = gll_tables()
    eye = np.eye(6)
    parts = [
        np.kron(np.kron(derivative, eye), eye),
        np.kron(np.kron(eye, derivative), eye),
        np.kron(np.kron(eye, eye), derivative),
    ]
    rows = class_rows()
    assert len(rows) == ROWS
    pick = np.zeros((ROWS, NAT))
    for at, node in enumerate(rows):
        if node is not None:
            pick[at, 36 * node[0] + 6 * node[1] + node[2]] = 1.0
    natural = np.zeros((3, ROWS, 256))
    from_class = np.zeros((3, ROWS, 256))
    back = np.zeros((ROWS, 768))
    divergence = np.zeros((ROWS, 768))
    squares = np.zeros((ROWS, 256))
    mass_class = pick @ mass
    for m in range(3):
        natural[m, :NAT, :NAT] = parts[m]
        from_class[m, :NAT, :ROWS] = parts[m] @ pick.T
        back[:, ROWS * m : ROWS * m + NAT] = pick @ parts[m].T
        divergence[:, ROWS * m : ROWS * m + NAT] = mass_class[:, None] * (pick @ parts[m])
        squares[:, :NAT] += pick @ (parts[m].astype(np.float32) ** 2).T
    to_natural = np.zeros((ROWS, 256))
    to_natural[:NAT, :ROWS] = pick.T
    mass_natural = np.zeros((ROWS,))
    mass_natural[:NAT] = mass
    pad = (pick.sum(1) == 0).astype(np.float32)
    out = []
    for matrix in (
        natural.reshape(3 * ROWS, 256),
        from_class.reshape(3 * ROWS, 256),
        back,
        divergence,
        squares,
    ):
        out += list(split_np(matrix))
    out.append(to_natural.astype(ml_dtypes.bfloat16))
    wide = lambda v: np.broadcast_to(v[:, None], (ROWS, 128)).astype(np.float32)
    out += [wide(mass_natural), wide(REACTION * mass_class), wide(pad)]
    lane = np.arange(128)[None, :] * np.ones((8, 1), int)
    sub = np.arange(8)[:, None] * np.ones((1, 128), int)
    ex, ey, ez = lane // 64, (lane // 32) % 2, lane % 32
    upper = sub >= 4
    corner_high = (sub % 4) == 2
    corner_low = (sub % 4) == 0
    masks = np.stack(
        [
            ex == 0,
            ex == 1,
            ey == 0,
            ey == 1,
            upper & (ey == 0),
            ~upper & (ey == 1),
            ez < 31,
            ez > 0,
            upper & (ez < 31),
            ~upper & (ez > 0),
            corner_high & (ez < 31),
            corner_low & (ez > 0),
            upper & (ey == 1),
            ~upper & (ey == 0),
            upper & (ey == 1) & (ex == 1),
            ~upper & (ey == 0) & (ex == 1),
            upper & (ey == 1) & (ex == 0),
            ~upper & (ey == 0) & (ex == 0),
        ]
    ).astype(np.float32)
    out.append(masks)
    side_x = [1, 0, 2, 0, 2, 1, 1]
    low_x = np.stack([(s == 0) & (ex == 0) for s in side_x])
    high_x = np.stack([(s == 2) & (ex == 1) for s in side_x])
    none = np.zeros((8, 128), bool)
    low_y = np.stack([none, none, none, ~upper & (ey == 0), ~upper & (ey == 0), ey == 0, none])
    high_y = np.stack([none, none, none, upper & (ey == 1), upper & (ey == 1), none, ey == 1])
    out.append(np.stack([low_x, high_x, low_y, high_y]).astype(np.float32))
    column = np.arange(256)
    place = np.zeros((3, DOM, 256))
    spread = np.zeros((3, 256, 128))
    lanes = np.arange(128)
    for fx in range(3):
        for dom in range(DOM):
            place[fx, dom] = (column // 8) == dom + fx - 1
        f = lanes % 16
        spread[fx] = (
            ((f // 3) == fx)[None, :]
            & (f < 9)[None, :]
            & ((column % 8)[:, None] == (lanes // 16 + f % 3 - 1)[None, :])
        )
    out.append(place.astype(np.float32))
    out.append(spread.reshape(768, 128).astype(ml_dtypes.bfloat16))
    return out


def dot(a, b):
    return jnp.dot(a, b, preferred_element_type=F32)


def halves(x):
    high = x.astype(BF16)
    low = (x - high.astype(F32)).astype(BF16)
    return high, low


def thirds(x):
    high = x.astype(BF16)
    rest = x - high.astype(F32)
    mid = rest.astype(BF16)
    low = (rest - mid.astype(F32)).astype(BF16)
    return high, mid, low


def product(high_ref, low_ref, x):
    depth = high_ref.shape[1]
    if x.shape[0] < depth:
        x = jnp.concatenate([x, jnp.zeros((depth - x.shape[0], x.shape[1]), F32)], axis=0)
    width = x.shape[1]
    high, low = halves(x)
    both = dot(high_ref[...], jnp.concatenate([high, low], axis=1))
    return both[:, :width] + both[:, width:] + dot(low_ref[...], high)


def pad_rows(x, rows):
    return jnp.concatenate([x, jnp.zeros((rows - x.shape[0], x.shape[1]), F32)], axis=0)


def move_lanes(x, select, transposed):
    rows = x.shape[0]
    stacked = jnp.concatenate(thirds(x), axis=0)
    if transposed:
        moved = lax.dot_general(
            stacked, select, (((1,), (1,)), ((), ())), preferred_element_type=F32
        )
    else:
        moved = dot(stacked, select)
    return moved[:rows] + moved[rows : 2 * rows] + moved[2 * rows :]


def roll(x, shift, axis):
    return pltpu.roll(x, shift, axis)


def cube(x):
    return x.reshape(x.shape[0] // 8, 8, 128)


def flat(x):
    return x.reshape(x.shape[0] * 8, 128)


def swap(x):
    return roll(x, 4, 1)


def block_sum(t, mask):
    inner, a0, a5, b0, b5, z0, z5 = (
        t[0:8],
        t[8:13],
        t[13:18],
        t[18:21],
        t[21:24],
        t[24:26],
        t[26:28],
    )
    a0, a5 = a0 + mask(1) * roll(a5, 64, 2), a5 + mask(0) * roll(a0, 64, 2)
    b0, b5 = b0 + mask(3) * roll(b5, 32, 2), b5 + mask(2) * roll(b0, 96, 2)
    edge = jnp.concatenate([a0[3:5], a5[3:5]], axis=0)
    turned = swap(edge)
    edge = edge + mask(4) * roll(turned, 96, 2) + mask(5) * roll(turned, 32, 2)
    z0, z5 = z0 + mask(7) * roll(z5, 1, 2), z5 + mask(6) * roll(z0, 127, 2)
    rim = jnp.concatenate([a0[2:3], a5[2:3], b0[2:3], b5[2:3]], axis=0)
    turned = swap(rim)
    rim = rim + mask(8) * roll(turned, 127, 2) + mask(9) * roll(turned, 1, 2)
    corner = jnp.concatenate([edge[1:2], edge[3:4]], axis=0)
    corner = (
        corner
        + mask(10) * roll(roll(corner, 2, 1), 127, 2)
        + mask(11) * roll(roll(corner, 6, 1), 1, 2)
    )
    return jnp.concatenate(
        [
            inner,
            a0[0:2],
            rim[0:1],
            edge[0:1],
            corner[0:1],
            a5[0:2],
            rim[1:2],
            edge[2:3],
            corner[1:2],
            b0[0:2],
            rim[2:3],
            b5[0:2],
            rim[3:4],
            z0,
            z5,
        ],
        axis=0,
    )


def add_neighbours(t, got, mask, has):
    left, right, down, up = has
    from_right, from_left, from_up, from_down, corners = got
    a0, a5, b0, b5 = t[8:13], t[13:18], t[18:21], t[21:24]
    a5 = a5 + (right * mask(1)) * roll(from_right, 64, 2)
    a0 = a0 + (left * mask(0)) * roll(from_left, 64, 2)
    b5 = b5 + (up * mask(3)) * roll(from_up[0:3], 32, 2)
    b0 = b0 + (down * mask(2)) * roll(from_down[0:3], 96, 2)
    up_rows = (up * mask(12)) * roll(swap(from_up[3:7]), 32, 2)
    down_rows = (down * mask(13)) * roll(swap(from_down[3:7]), 96, 2)
    edge = up_rows + down_rows
    e0 = a0[3:5] + edge[0:2]
    e5 = a5[3:5] + edge[2:4]
    e5 = e5 + (right * up * mask(14)) * roll(swap(corners[0]), 96, 2)
    e5 = e5 + (right * down * mask(15)) * roll(swap(corners[1]), 32, 2)
    e0 = e0 + (left * up * mask(16)) * roll(swap(corners[2]), 96, 2)
    e0 = e0 + (left * down * mask(17)) * roll(swap(corners[3]), 32, 2)
    return jnp.concatenate([t[0:8], a0[0:3], e0, a5[0:3], e5, b0, b5, t[24:28]], axis=0)


def by_kind(t):
    total = lambda *spans: sum(jnp.sum(t[a:b], axis=0, keepdims=True) for a, b in spans)
    return jnp.concatenate(
        [
            total((0, 8), (24, 28)),
            total((8, 11)),
            total((13, 16)),
            total((11, 13)),
            total((16, 18)),
            total((18, 21)),
            total((21, 24)),
        ],
        axis=0,
    )


def from_kinds(v):
    order = [0] * 8 + [1] * 3 + [3] * 2 + [2] * 3 + [4] * 2 + [5] * 3 + [6] * 3 + [0] * 4
    return jnp.concatenate([v[k : k + 1] for k in order], axis=0)


def total_of(x):
    return jnp.sum(jnp.sum(x, axis=0, keepdims=True), axis=2, keepdims=True)


NAMES = (
    "vel",
    "base",
    "visc",
    "order",
    "coarse",
    "nat_hi",
    "nat_lo",
    "cls_hi",
    "cls_lo",
    "back_hi",
    "back_lo",
    "div_hi",
    "div_lo",
    "sq_hi",
    "sq_lo",
    "out_pick",
    "mass",
    "react",
    "pad",
    "mask",
    "side",
    "place",
    "spread",
)
ORDER = (
    "nat_hi",
    "vel",
    "base",
    "nat_lo",
    "div_hi",
    "div_lo",
    "order",
    "visc",
    "mask",
    "side",
    "mass",
    "sq_hi",
    "sq_lo",
    "react",
    "coarse",
    "place",
    "spread",
    "pad",
    "cls_hi",
    "cls_lo",
    "back_hi",
    "back_lo",
    "out_pick",
)


def kernel(*refs):
    count = len(NAMES)
    sources = dict(zip(NAMES, refs[:count]))
    lin_ref, press_ref = refs[count : count + 2]
    held = dict(zip(NAMES, refs[count + 2 : 2 * count + 2]))
    (
        load_sem,
        field,
        y_up,
        y_down,
        got_x,
        got_y,
        got_c,
        row_a,
        row_b,
        all_a,
        all_b,
        weight_ref,
        solve_ref,
        send_h,
        recv_h,
        send_a,
        recv_a,
        send_b,
        recv_b,
    ) = refs[2 * count + 2 :]
    loads = {
        name: pltpu.make_async_copy(sources[name], held[name], load_sem.at[at])
        for at, name in enumerate(NAMES)
    }
    for name in ORDER:
        loads[name].start()
    ready = set()

    def need(name):
        if name not in ready:
            loads[name].wait()
            ready.add(name)
        return held[name]

    dom = lax.axis_index("dom")
    sub = lax.axis_index("sub")
    dom_next, dom_prev = lax.rem(dom + 1, DOM), lax.rem(dom + DOM - 1, DOM)
    sub_next, sub_prev = lax.rem(sub + 1, SUB), lax.rem(sub + SUB - 1, SUB)
    barrier = pltpu.get_barrier_semaphore()

    def greet(where):
        pl.semaphore_signal(barrier, inc=1, device_id=where, device_id_type=MESH)

    core = lax.rem(sub, 2)
    chip_x = lax.div(sub, 2)
    chip_y = lax.div(dom, 8)
    chip_z = lax.rem(dom, 8)
    row_starts = [8 * lax.rem(chip_y + step, 4) for step in (2, 1, 3, 0)]
    columns = [lax.rem(sub + 2 * step, SUB) for step in (2, 1, 3, 0)]

    def each_chip(visit):
        @pl.loop(0, 7)
        def _(n):
            step = 4 + (1 - 2 * lax.rem(n, 2)) * lax.div(n + 1, 2)
            z = lax.rem(chip_z + step, 8)
            for start in row_starts:
                for column in columns:
                    visit((start + z, column))

        for start in row_starts:
            for column in columns:
                if start is not row_starts[3] or column is not columns[3]:
                    visit((start + chip_z, column))

    partner = (dom, sub + 1 - 2 * core)

    each_chip(greet)
    greet(partner)
    greet((dom, jnp.where(core == 0, sub_prev, sub_next)))
    diagonals = (
        (dom_prev, sub_prev),
        (dom_prev, sub_next),
        (dom_next, sub_prev),
        (dom_next, sub_next),
    )
    for where in diagonals:
        greet(where)

    mask = lambda at: need("mask")[at]

    def flag(condition):
        return jnp.where(condition, 1.0, 0.0).astype(F32)

    has = (flag(dom > 0), flag(dom < DOM - 1), flag(sub > 0), flag(sub < SUB - 1))

    vel = [pad_rows(need("vel")[c], ROWS) for c in range(3)]
    base = [pad_rows(need("base")[c], ROWS) for c in range(3)]
    advect = []
    for c in range(3):
        grads = product(need("nat_hi"), need("nat_lo"), jnp.concatenate([vel[c], base[c]], axis=1))
        acc = jnp.zeros((ROWS, 128), F32)
        for m in range(3):
            part = grads[ROWS * m : ROWS * (m + 1)]
            acc = acc - base[m] * part[:, :128] - vel[m] * part[:, 128:]
        advect.append(acc)
        lin_ref[c] = acc[:NAT]
    select = jnp.where(
        lax.broadcasted_iota(jnp.int32, (128, 128), 0) == need("order")[...], 1.0, 0.0
    ).astype(BF16)
    moved = move_lanes(
        jnp.concatenate(
            [
                product(need("div_hi"), need("div_lo"), jnp.concatenate(advect, axis=0)),
                pad_rows(need("visc")[...], ROWS),
            ],
            axis=0,
        ),
        select,
        True,
    )
    rhs_own = cube(moved[:ROWS])
    weighted = need("mass")[...] * moved[ROWS:]
    weight_ref[...] = jnp.concatenate([weighted, weighted, weighted], axis=0)
    diag_own = cube(need("react")[...] + product(need("sq_hi"), need("sq_lo"), weighted))

    left, right, down, up = has
    side_l, side_r = (0.5 * left) * need("side")[0], (0.5 * right) * need("side")[1]
    side_d, side_u = (0.5 * down) * need("side")[2], (0.5 * up) * need("side")[3]
    along_x = (side_l, 1.0 - side_l - side_r, side_r)
    along_y = (side_d, 1.0 - side_d - side_u, side_u)

    def coarse_parts(kinds):
        return [
            jnp.sum(along_x[fx] * along_y[fy] * kinds, axis=0, keepdims=True)
            for fx in range(3)
            for fy in range(3)
        ]

    def spread_coarse(solved):
        values = 0.0
        for fx in range(3):
            inner = sum(solved[3 * fx + fy] * along_y[fy] for fy in range(3))
            values = values + along_x[fx] * inner
        return from_kinds(values)

    lane = lax.broadcasted_iota(jnp.int32, (16, 128), 1)
    slot = lax.broadcasted_iota(jnp.int32, (16, 128), 0)
    home = lane == 16 * sub + slot

    def send(src, dst, send_sem, recv_sem, where):
        pltpu.make_async_remote_copy(
            src_ref=src,
            dst_ref=dst,
            send_sem=send_sem,
            recv_sem=recv_sem,
            device_id=where,
            device_id_type=MESH,
        ).start()

    def wait_for(ref, sem):
        pltpu.make_async_copy(ref, ref, sem).wait()

    def start_gather(at, partials):
        count = len(partials)
        stack = jnp.concatenate(partials, axis=0)
        sums = jnp.sum(jnp.sum(stack, axis=1), axis=1, keepdims=True)
        if count < 16:
            sums = jnp.concatenate([sums, jnp.zeros((16 - count, 1), F32)], axis=0)
        row = jnp.sum(jnp.where(home, sums, 0.0), axis=0, keepdims=True)
        row_a[at] = row
        send(row_a.at[at], all_a.at[at], send_a.at[at], recv_a.at[at], partner)
        return row

    def forward_gather(at, row):
        wait_for(all_a.at[at], recv_a.at[at])
        row = row + all_a[at]
        row_b[at] = row
        here = DOM * chip_x + dom

        each_chip(
            functools.partial(
                send, row_b.at[at], all_b.at[at, here], send_b.at[at], recv_b.at[at]
            )
        )
        all_b[at, here] = row

    def finish_gather(at):
        wait_for(all_b.at[at, 0 : CHIPS - 1], recv_b.at[at])
        return jnp.sum(all_b[at].reshape(4, DOM, 128), axis=0)

    def start_halo(at, which, own):
        t = block_sum(own, mask)
        field[at] = t
        y_up[at, 0:3] = t[21:24]
        y_up[at, 3:5] = t[11:13]
        y_up[at, 5:7] = t[16:18]
        y_down[at, 0:3] = t[18:21]
        y_down[at, 3:5] = t[11:13]
        y_down[at, 5:7] = t[16:18]
        ss, rs = send_h.at[which], recv_h.at[which]
        send(field.at[at, 8:13], got_x.at[at, 0], ss.at[0], rs.at[0], (dom_prev, sub))
        send(field.at[at, 13:18], got_x.at[at, 1], ss.at[0], rs.at[0], (dom_next, sub))
        send(y_down.at[at], got_y.at[at, 0], ss.at[1], rs.at[1], (dom, sub_prev))
        send(y_up.at[at], got_y.at[at, 1], ss.at[1], rs.at[1], (dom, sub_next))
        for n, where in enumerate(diagonals):
            src = field.at[at, 11:13] if n < 2 else field.at[at, 16:18]
            send(src, got_c.at[at, n], ss.at[2], rs.at[2], where)
        return t

    def finish_halo(at, which, t):
        rs = recv_h.at[which]
        wait_for(got_x.at[at], rs.at[0])
        wait_for(got_y.at[at], rs.at[1])
        wait_for(got_c.at[at], rs.at[2])
        got = (
            got_x[at, 0],
            got_x[at, 1],
            got_y[at, 0],
            got_y[at, 1],
            [got_c[at, n] for n in range(4)],
        )
        return add_neighbours(t, got, mask, has)

    def apply(u):
        v = flat(u)
        g = product(need("cls_hi"), need("cls_lo"), v)
        h = pad_rows(g * weight_ref[...], 768)
        return cube(product(need("back_hi"), need("back_lo"), h) + need("react")[...] * v)

    def inner(a, b):
        return jnp.sum(a * b, axis=0, keepdims=True)

    def results(everyone, dots):
        rows = cube(everyone)
        terms = [
            jnp.sum(rows * cube(solve_ref[a]), axis=0, keepdims=True) for a in range(NFACE)
        ]
        column = jnp.sum(rows, axis=0, keepdims=True)
        which = lax.broadcasted_iota(jnp.int32, (1, 8, 128), 2) % 16
        terms += [jnp.where(which == NFACE + d, column, 0.0) for d in range(dots)]
        sums = jnp.sum(
            jnp.sum(jnp.concatenate(terms, axis=0), axis=1, keepdims=True), axis=2, keepdims=True
        )
        return [sums[n] for n in range(NFACE + dots)]

    pl.semaphore_wait(barrier, CHIPS - 1 + 2 + 4)
    row = start_gather(0, coarse_parts(by_kind(rhs_own)))
    rhs_block = start_halo(0, 0, rhs_own)
    diag_block = start_halo(1, 1, diag_own)

    chosen = []
    for ax in (-1, 0, 1):
        for ay in (-1, 0, 1):
            at = jnp.clip((dom + ax) * SUB + sub + ay, 0, DOM * SUB - 1)
            chosen.append(need("coarse")[pl.ds(at, 1), :])
    for a in range(NFACE):
        wide = jnp.concatenate([need("place")[fx] * chosen[a] for fx in range(3)], axis=1)
        pieces = thirds(wide)
        solve_ref[a] = sum(dot(piece, need("spread")[...]) for piece in pieces)

    forward_gather(0, row)
    r_all = finish_halo(0, 0, rhs_block)
    d_all = finish_halo(1, 1, diag_block)
    inverse = 1.0 / (d_all + cube(need("pad")[...]))
    solved = results(finish_gather(0), 0)
    r_own = rhs_own
    z = inverse * r_all + spread_coarse(solved)

    direction = None
    for it in range(3):
        w_own = apply(z)
        dots = [inner(z, r_own), inner(z, w_own)]
        last = it == 2
        parts = coarse_parts(by_kind(w_own)) if not last else [jnp.zeros((1, 8, 128), F32)] * 9
        row = start_gather(it + 1, parts + dots)
        if not last:
            w_block = start_halo(it + 2, it + 2, w_own)
        forward_gather(it + 1, row)
        if not last:
            w_all = finish_halo(it + 2, it + 2, w_block)
        got = results(finish_gather(it + 1), 2)
        gamma, curve = got[NFACE], got[NFACE + 1]
        solved_w = got[:NFACE]
        if it == 0:
            alpha = gamma / curve
            direction = z
            q = alpha * direction
            if not last:
                along_own, along_all, along_solved = w_own, w_all, solved_w
        else:
            beta = gamma / gamma_before
            alpha = gamma / (curve - beta * gamma / alpha)
            direction = z + beta * direction
            q = q + alpha * direction
            if not last:
                along_own = w_own + beta * along_own
                along_all = w_all + beta * along_all
                along_solved = [a + beta * b for a, b in zip(solved_w, along_solved)]
        gamma_before = gamma
        if not last:
            r_own = r_own - alpha * along_own
            r_all = r_all - alpha * along_all
            solved = [a - alpha * b for a, b in zip(solved, along_solved)]
            z = inverse * r_all + spread_coarse(solved)

    slots = pad_rows(move_lanes(flat(q), select, False), 256)
    press_ref[...] = sum(dot(need("out_pick")[...], piece) for piece in thirds(slots))[:NAT]
    grads = product(need("cls_hi"), need("cls_lo"), slots)
    for c in range(3):
        lin_ref[c] = lin_ref[c] - grads[ROWS * c : ROWS * c + NAT]

    for at in range(4):
        wait_for(all_a.at[at], send_a.at[at])
        wait_for(all_b.at[at, 0 : CHIPS - 1], send_b.at[at])
        wait_for(got_x.at[at], send_h.at[at, 0])
        wait_for(got_y.at[at], send_h.at[at, 1])
        wait_for(got_c.at[at], send_h.at[at, 2])


def shards(velocity, base_flow, viscosity, cell_order, coarse_inv):
    args = [velocity, base_flow, viscosity, cell_order, coarse_inv]
    args += [jnp.asarray(t) for t in tables()]
    vmem = pl.BlockSpec(memory_space=pltpu.VMEM)
    hbm = pl.BlockSpec(memory_space=pltpu.HBM)
    dma = pltpu.SemaphoreType.DMA
    return pl.pallas_call(
        kernel,
        out_shape=(
            pltpu.VMEM((3, NAT, 128), F32),
            pltpu.VMEM((NAT, 128), F32),
        ),
        in_specs=[hbm] * len(args),
        out_specs=(vmem, vmem),
        scratch_shapes=[pltpu.VMEM(arg.shape, arg.dtype) for arg in args]
        + [
            dma((len(args),)),
            pltpu.VMEM((4, 28, 8, 128), F32),
            pltpu.VMEM((4, 7, 8, 128), F32),
            pltpu.VMEM((4, 7, 8, 128), F32),
            pltpu.VMEM((4, 2, 5, 8, 128), F32),
            pltpu.VMEM((4, 2, 7, 8, 128), F32),
            pltpu.VMEM((4, 4, 2, 8, 128), F32),
            pltpu.VMEM((4, 1, 128), F32),
            pltpu.VMEM((4, 1, 128), F32),
            pltpu.VMEM((4, 1, 128), F32),
            pltpu.VMEM((4, CHIPS, 1, 128), F32),
            pltpu.VMEM((3 * ROWS, 128), F32),
            pltpu.VMEM((NFACE, DOM, 128), F32),
            dma((4, 3)),
            dma((4, 3)),
            dma((4,)),
            dma((4,)),
            dma((4,)),
            dma((4,)),
        ],
        compiler_params=pltpu.CompilerParams(
            collective_id=0, has_side_effects=True, vmem_limit_bytes=40 << 20
        ),
    )(*[pltpu.with_memory_space_constraint(arg, pltpu.HBM) for arg in args])


def solution(mesh):
    placed = (
        P(None, None, ("dom", "sub")),
        P(None, None, ("dom", "sub")),
        P(None, ("dom", "sub")),
        P(("dom", "sub"), None),
        P(),
    )
    return jax.shard_map(
        shards,
        mesh=mesh,
        in_specs=placed,
        out_specs=(P(None, None, ("dom", "sub")), P(None, ("dom", "sub"))),
        check_vma=False,
    )
```

```python
import functools

import jax
import jax.numpy as jnp
import ml_dtypes
import numpy as np
from jax import lax
from jax.experimental import pallas as pl
from jax.experimental.pallas import tpu as pltpu
from jax.sharding import PartitionSpec as P

F32 = jnp.float32
BF16 = jnp.bfloat16
MESH = pl.DeviceIdType.MESH
REACTION = 0.001
DOM = 32
SUB = 8
CHIPS = 128
ROWS = 224
NAT = 216
NFACE = 9
MESSAGE_ROWS = (1, 1, 2, 2)


def gll_tables():
    points = np.array(
        [
            -1.0,
            -0.7650553239294647,
            -0.2852315164806451,
            0.2852315164806451,
            0.7650553239294647,
            1.0,
        ]
    )
    weights = np.array(
        [
            1.0 / 15.0,
            0.378474956297847,
            0.5548583770354862,
            0.5548583770354862,
            0.378474956297847,
            1.0 / 15.0,
        ]
    )
    legendre = (63.0 * points**5 - 70.0 * points**3 + 15.0 * points) / 8.0
    derivative = np.zeros((6, 6))
    for a in range(6):
        for b in range(6):
            if a != b:
                derivative[a, b] = legendre[a] / (legendre[b] * (points[a] - points[b]))
    derivative[0, 0] = -7.5
    derivative[5, 5] = 7.5
    mass = weights[:, None, None] * weights[None, :, None] * weights[None, None, :]
    return (
        derivative.astype(np.float32).astype(np.float64),
        mass.astype(np.float32).astype(np.float64).reshape(-1),
    )


def class_rows():
    mid = (1, 2, 3, 4)
    rows = [(i, j, k) for i in mid for j in mid for k in mid]
    for i in (0, 5):
        rows += [(i, j, k) for j in mid for k in mid]
        rows += [(i, j, k) for k in (0, 5) for j in mid]
        rows += [(i, j, k) for j in (0, 5) for k in mid]
        for j in (0, 5):
            for k in (0, 5):
                rows += [(i, j, k), None]
    for j in (0, 5):
        rows += [(i, j, k) for i in mid for k in mid]
        rows += [(i, j, k) for k in (0, 5) for i in mid]
    for k in (0, 5):
        rows += [(i, j, k) for i in mid for j in mid]
    return rows


def split_np(matrix):
    single = matrix.astype(np.float32)
    high = single.astype(ml_dtypes.bfloat16)
    low = (single - high.astype(np.float32)).astype(ml_dtypes.bfloat16)
    return high, low


def tables():
    derivative, mass = gll_tables()
    eye = np.eye(6)
    parts = [
        np.kron(np.kron(derivative, eye), eye),
        np.kron(np.kron(eye, derivative), eye),
        np.kron(np.kron(eye, eye), derivative),
    ]
    rows = class_rows()
    assert len(rows) == ROWS
    pick = np.zeros((ROWS, NAT))
    for at, node in enumerate(rows):
        if node is not None:
            pick[at, 36 * node[0] + 6 * node[1] + node[2]] = 1.0
    natural = np.zeros((3, ROWS, 256))
    from_class = np.zeros((3, ROWS, 256))
    back = np.zeros((ROWS, 768))
    divergence = np.zeros((ROWS, 768))
    squares = np.zeros((ROWS, 256))
    mass_class = pick @ mass
    for m in range(3):
        natural[m, :NAT, :NAT] = parts[m]
        from_class[m, :NAT, :ROWS] = parts[m] @ pick.T
        back[:, ROWS * m : ROWS * m + NAT] = pick @ parts[m].T
        divergence[:, ROWS * m : ROWS * m + NAT] = mass_class[:, None] * (pick @ parts[m])
        squares[:, :NAT] += pick @ (parts[m].astype(np.float32) ** 2).T
    to_natural = np.zeros((ROWS, 256))
    to_natural[:NAT, :ROWS] = pick.T
    mass_natural = np.zeros((ROWS,))
    mass_natural[:NAT] = mass
    pad = (pick.sum(1) == 0).astype(np.float32)
    out = []
    for matrix in (
        natural.reshape(3 * ROWS, 256),
        from_class.reshape(3 * ROWS, 256),
        back,
        divergence,
        squares,
    ):
        out += list(split_np(matrix))
    out.append(to_natural.astype(ml_dtypes.bfloat16))
    wide = lambda v: np.broadcast_to(v[:, None], (ROWS, 128)).astype(np.float32)
    out += [wide(mass_natural), wide(REACTION * mass_class), wide(pad)]
    lane = np.arange(128)[None, :] * np.ones((8, 1), int)
    sub = np.arange(8)[:, None] * np.ones((1, 128), int)
    ex, ey, ez = lane // 64, (lane // 32) % 2, lane % 32
    upper = sub >= 4
    corner_high = (sub % 4) == 2
    corner_low = (sub % 4) == 0
    masks = np.stack(
        [
            ex == 0,
            ex == 1,
            ey == 0,
            ey == 1,
            upper & (ey == 0),
            ~upper & (ey == 1),
            ez < 31,
            ez > 0,
            upper & (ez < 31),
            ~upper & (ez > 0),
            corner_high & (ez < 31),
            corner_low & (ez > 0),
            upper & (ey == 1),
            ~upper & (ey == 0),
            upper & (ey == 1) & (ex == 1),
            ~upper & (ey == 0) & (ex == 1),
            upper & (ey == 1) & (ex == 0),
            ~upper & (ey == 0) & (ex == 0),
        ]
    ).astype(np.float32)
    out.append(masks)
    side_x = [1, 0, 2, 0, 2, 1, 1]
    low_x = np.stack([(s == 0) & (ex == 0) for s in side_x])
    high_x = np.stack([(s == 2) & (ex == 1) for s in side_x])
    none = np.zeros((8, 128), bool)
    low_y = np.stack([none, none, none, ~upper & (ey == 0), ~upper & (ey == 0), ey == 0, none])
    high_y = np.stack([none, none, none, upper & (ey == 1), upper & (ey == 1), none, ey == 1])
    out.append(np.stack([low_x, high_x, low_y, high_y]).astype(np.float32))
    column = np.arange(256)
    place = np.zeros((3, DOM, 256))
    spread = np.zeros((3, 256, 128))
    lanes = np.arange(128)
    for fx in range(3):
        for dom in range(DOM):
            place[fx, dom] = (column // 8) == dom + fx - 1
        f = lanes % 16
        spread[fx] = (
            ((f // 3) == fx)[None, :]
            & (f < 9)[None, :]
            & ((column % 8)[:, None] == (lanes // 16 + f % 3 - 1)[None, :])
        )
    out.append(place.astype(np.float32))
    pairs = coarse_pairs()
    firsts = np.zeros((3, 256, 256))
    seconds = np.zeros((3, 256, 256))
    slots = np.full((2, 88, 128), -1000, np.int32)
    for at, (f, g) in enumerate(pairs):
        group, inside = at // 16, at % 16
        slots[group, 9 * f + g] = inside
        for sub in range(SUB):
            column_at = 128 * group + 16 * sub + inside
            firsts[f // 3, :, column_at] = ((column % 8) == sub + f % 3 - 1) * (1 + (f != g))
            seconds[g // 3, :, column_at] = (column % 8) == sub + g % 3 - 1
    unfold = np.concatenate([spread, firsts, seconds], axis=2)
    out.append(spread.reshape(768, 128).astype(ml_dtypes.bfloat16))
    out.append(unfold.reshape(768, 640).astype(ml_dtypes.bfloat16))
    out.append(slots)
    return out


def coarse_pairs():
    return [
        (f, g)
        for f in range(NFACE)
        for g in range(f, NFACE)
        if abs(f // 3 - g // 3) < 2 and abs(f % 3 - g % 3) < 2
    ]


def dot(a, b):
    return jnp.dot(a, b, preferred_element_type=F32)


def halves(x):
    high = x.astype(BF16)
    low = (x - high.astype(F32)).astype(BF16)
    return high, low


def thirds(x):
    high = x.astype(BF16)
    rest = x - high.astype(F32)
    mid = rest.astype(BF16)
    low = (rest - mid.astype(F32)).astype(BF16)
    return high, mid, low


def product(high_ref, low_ref, x):
    depth = high_ref.shape[1]
    if x.shape[0] < depth:
        x = jnp.concatenate([x, jnp.zeros((depth - x.shape[0], x.shape[1]), F32)], axis=0)
    width = x.shape[1]
    high, low = halves(x)
    both = dot(high_ref[...], jnp.concatenate([high, low], axis=1))
    return both[:, :width] + both[:, width:] + dot(low_ref[...], high)


def pad_rows(x, rows):
    return jnp.concatenate([x, jnp.zeros((rows - x.shape[0], x.shape[1]), F32)], axis=0)


def move_lanes(x, select, transposed):
    rows = x.shape[0]
    stacked = jnp.concatenate(thirds(x), axis=0)
    if transposed:
        moved = lax.dot_general(
            stacked, select, (((1,), (1,)), ((), ())), preferred_element_type=F32
        )
    else:
        moved = dot(stacked, select)
    return moved[:rows] + moved[rows : 2 * rows] + moved[2 * rows :]


def roll(x, shift, axis):
    return pltpu.roll(x, shift, axis)


def cube(x):
    return x.reshape(x.shape[0] // 8, 8, 128)


def flat(x):
    return x.reshape(x.shape[0] * 8, 128)


def swap(x):
    return roll(x, 4, 1)


def block_sum(t, mask):
    inner, a0, a5, b0, b5, z0, z5 = (
        t[0:8],
        t[8:13],
        t[13:18],
        t[18:21],
        t[21:24],
        t[24:26],
        t[26:28],
    )
    a0, a5 = a0 + mask(1) * roll(a5, 64, 2), a5 + mask(0) * roll(a0, 64, 2)
    b0, b5 = b0 + mask(3) * roll(b5, 32, 2), b5 + mask(2) * roll(b0, 96, 2)
    edge = jnp.concatenate([a0[3:5], a5[3:5]], axis=0)
    turned = swap(edge)
    edge = edge + mask(4) * roll(turned, 96, 2) + mask(5) * roll(turned, 32, 2)
    z0, z5 = z0 + mask(7) * roll(z5, 1, 2), z5 + mask(6) * roll(z0, 127, 2)
    rim = jnp.concatenate([a0[2:3], a5[2:3], b0[2:3], b5[2:3]], axis=0)
    turned = swap(rim)
    rim = rim + mask(8) * roll(turned, 127, 2) + mask(9) * roll(turned, 1, 2)
    corner = jnp.concatenate([edge[1:2], edge[3:4]], axis=0)
    corner = (
        corner
        + mask(10) * roll(roll(corner, 2, 1), 127, 2)
        + mask(11) * roll(roll(corner, 6, 1), 1, 2)
    )
    return jnp.concatenate(
        [
            inner,
            a0[0:2],
            rim[0:1],
            edge[0:1],
            corner[0:1],
            a5[0:2],
            rim[1:2],
            edge[2:3],
            corner[1:2],
            b0[0:2],
            rim[2:3],
            b5[0:2],
            rim[3:4],
            z0,
            z5,
        ],
        axis=0,
    )


def add_neighbours(t, got, mask, has):
    left, right, down, up = has
    from_right, from_left, from_up, from_down, corners = got
    a0, a5, b0, b5 = t[8:13], t[13:18], t[18:21], t[21:24]
    a5 = a5 + (right * mask(1)) * roll(from_right, 64, 2)
    a0 = a0 + (left * mask(0)) * roll(from_left, 64, 2)
    b5 = b5 + (up * mask(3)) * roll(from_up[0:3], 32, 2)
    b0 = b0 + (down * mask(2)) * roll(from_down[0:3], 96, 2)
    up_rows = (up * mask(12)) * roll(swap(from_up[3:7]), 32, 2)
    down_rows = (down * mask(13)) * roll(swap(from_down[3:7]), 96, 2)
    edge = up_rows + down_rows
    e0 = a0[3:5] + edge[0:2]
    e5 = a5[3:5] + edge[2:4]
    e5 = e5 + (right * up * mask(14)) * roll(swap(corners[0]), 96, 2)
    e5 = e5 + (right * down * mask(15)) * roll(swap(corners[1]), 32, 2)
    e0 = e0 + (left * up * mask(16)) * roll(swap(corners[2]), 96, 2)
    e0 = e0 + (left * down * mask(17)) * roll(swap(corners[3]), 32, 2)
    return jnp.concatenate([t[0:8], a0[0:3], e0, a5[0:3], e5, b0, b5, t[24:28]], axis=0)


def by_kind(t):
    total = lambda *spans: sum(jnp.sum(t[a:b], axis=0, keepdims=True) for a, b in spans)
    return jnp.concatenate(
        [
            total((0, 8), (24, 28)),
            total((8, 11)),
            total((13, 16)),
            total((11, 13)),
            total((16, 18)),
            total((18, 21)),
            total((21, 24)),
        ],
        axis=0,
    )


def from_kinds(v):
    order = [0] * 8 + [1] * 3 + [3] * 2 + [2] * 3 + [4] * 2 + [5] * 3 + [6] * 3 + [0] * 4
    return jnp.concatenate([v[k : k + 1] for k in order], axis=0)


def total_of(x):
    return jnp.sum(jnp.sum(x, axis=0, keepdims=True), axis=2, keepdims=True)


NAMES = (
    "vel",
    "base",
    "visc",
    "order",
    "coarse",
    "nat_hi",
    "nat_lo",
    "cls_hi",
    "cls_lo",
    "back_hi",
    "back_lo",
    "div_hi",
    "div_lo",
    "sq_hi",
    "sq_lo",
    "out_pick",
    "mass",
    "react",
    "pad",
    "mask",
    "side",
    "place",
    "spread",
    "unfold",
    "slots",
)
ORDER = (
    "nat_hi",
    "vel",
    "base",
    "nat_lo",
    "div_hi",
    "div_lo",
    "order",
    "visc",
    "mask",
    "side",
    "mass",
    "sq_hi",
    "sq_lo",
    "react",
    "coarse",
    "place",
    "spread",
    "pad",
    "cls_hi",
    "cls_lo",
    "back_hi",
    "back_lo",
    "unfold",
    "slots",
    "out_pick",
)


def kernel(*refs):
    count = len(NAMES)
    sources = dict(zip(NAMES, refs[:count]))
    lin_ref, press_ref = refs[count : count + 2]
    held = dict(zip(NAMES, refs[count + 2 : 2 * count + 2]))
    (
        load_sem,
        field,
        y_up,
        y_down,
        got_x,
        got_y,
        got_c,
        row_a0,
        row_a1,
        row_a2,
        row_a3,
        row_b0,
        row_b1,
        row_b2,
        row_b3,
        all_a0,
        all_a1,
        all_a2,
        all_a3,
        all_b0,
        all_b1,
        all_b2,
        all_b3,
        weight_ref,
        solve_ref,
        phi_ref,
        entry_ref,
        coarse_hi,
        coarse_lo,
        send_h,
        recv_h,
        send_a,
        recv_a,
        send_b,
        recv_b,
    ) = refs[2 * count + 2 :]
    row_a = (row_a0, row_a1, row_a2, row_a3)
    row_b = (row_b0, row_b1, row_b2, row_b3)
    all_a = (all_a0, all_a1, all_a2, all_a3)
    all_b = (all_b0, all_b1, all_b2, all_b3)
    loads = {
        name: pltpu.make_async_copy(sources[name], held[name], load_sem.at[at])
        for at, name in enumerate(NAMES)
    }
    for name in ORDER[:4]:
        loads[name].start()
    ready = set()

    def need(name):
        if name not in ready:
            loads[name].wait()
            ready.add(name)
        return held[name]

    dom = lax.axis_index("dom")
    sub = lax.axis_index("sub")
    dom_next, dom_prev = lax.rem(dom + 1, DOM), lax.rem(dom + DOM - 1, DOM)
    sub_next, sub_prev = lax.rem(sub + 1, SUB), lax.rem(sub + SUB - 1, SUB)
    barrier = pltpu.get_barrier_semaphore()

    def greet(where):
        pl.semaphore_signal(barrier, inc=1, device_id=where, device_id_type=MESH)

    core = lax.rem(sub, 2)
    chip_x = lax.div(sub, 2)
    chip_y = lax.div(dom, 8)
    chip_z = lax.rem(dom, 8)
    row_starts = [8 * lax.rem(chip_y + step, 4) for step in (2, 1, 3, 0)]
    columns = [lax.rem(sub + 2 * step, SUB) for step in (2, 1, 3, 0)]

    def each_chip(visit):
        @pl.loop(0, 7)
        def _(n):
            step = 4 + (1 - 2 * lax.rem(n, 2)) * lax.div(n + 1, 2)
            z = lax.rem(chip_z + step, 8)
            for start in row_starts:
                for column in columns:
                    visit((start + z, column))

        for start in row_starts:
            for column in columns:
                if start is not row_starts[3] or column is not columns[3]:
                    visit((start + chip_z, column))

    partner = (dom, sub + 1 - 2 * core)

    each_chip(greet)
    greet(partner)
    greet((dom, jnp.where(core == 0, sub_prev, sub_next)))
    diagonals = (
        (dom_prev, sub_prev),
        (dom_prev, sub_next),
        (dom_next, sub_prev),
        (dom_next, sub_next),
    )
    for where in diagonals:
        greet(where)
    for name in ORDER[4:]:
        loads[name].start()

    mask = lambda at: need("mask")[at]

    def flag(condition):
        return jnp.where(condition, 1.0, 0.0).astype(F32)

    has = (flag(dom > 0), flag(dom < DOM - 1), flag(sub > 0), flag(sub < SUB - 1))

    vel = [pad_rows(need("vel")[c], ROWS) for c in range(3)]
    base = [pad_rows(need("base")[c], ROWS) for c in range(3)]
    advect = []
    for c in range(3):
        grads = product(need("nat_hi"), need("nat_lo"), jnp.concatenate([vel[c], base[c]], axis=1))
        acc = jnp.zeros((ROWS, 128), F32)
        for m in range(3):
            part = grads[ROWS * m : ROWS * (m + 1)]
            acc = acc - base[m] * part[:, :128] - vel[m] * part[:, 128:]
        advect.append(acc)
        lin_ref[c] = acc[:NAT]
    select = jnp.where(
        lax.broadcasted_iota(jnp.int32, (128, 128), 0) == need("order")[...], 1.0, 0.0
    ).astype(BF16)
    rhs_own = cube(
        move_lanes(
            product(need("div_hi"), need("div_lo"), jnp.concatenate(advect, axis=0)), select, True
        )
    )

    left, right, down, up = has
    side_l, side_r = (0.5 * left) * need("side")[0], (0.5 * right) * need("side")[1]
    side_d, side_u = (0.5 * down) * need("side")[2], (0.5 * up) * need("side")[3]
    along_x = (side_l, 1.0 - side_l - side_r, side_r)
    along_y = (side_d, 1.0 - side_d - side_u, side_u)

    def coarse_parts(kinds):
        return [
            jnp.sum(along_x[fx] * along_y[fy] * kinds, axis=0, keepdims=True)
            for fx in range(3)
            for fy in range(3)
        ]

    def spread_coarse(solved):
        values = 0.0
        for fx in range(3):
            inner = sum(solved[3 * fx + fy] * along_y[fy] for fy in range(3))
            values = values + along_x[fx] * inner
        return from_kinds(values)

    lane = lax.broadcasted_iota(jnp.int32, (16, 128), 1)
    slot = lax.broadcasted_iota(jnp.int32, (16, 128), 0)
    home = lane == 16 * sub + slot

    def send(src, dst, send_sem, recv_sem, where):
        pltpu.make_async_remote_copy(
            src_ref=src,
            dst_ref=dst,
            send_sem=send_sem,
            recv_sem=recv_sem,
            device_id=where,
            device_id_type=MESH,
        ).start()

    def wait_for(ref, sem):
        pltpu.make_async_copy(ref, ref, sem).wait()

    def packed(partials):
        count = len(partials)
        stack = jnp.concatenate(partials, axis=0)
        sums = jnp.sum(jnp.sum(stack, axis=1), axis=1, keepdims=True)
        if count < 16:
            sums = jnp.concatenate([sums, jnp.zeros((16 - count, 1), F32)], axis=0)
        return jnp.sum(jnp.where(home, sums, 0.0), axis=0, keepdims=True)

    def start_gather(at, rows):
        for n, row in enumerate(rows):
            row_a[at][n] = row
        send(row_a[at], all_a[at], send_a.at[at], recv_a.at[at], partner)

    def forward_gather(at, rows):
        wait_for(all_a[at], recv_a.at[at])
        here = DOM * chip_x + dom
        rows = [row + all_a[at][n] for n, row in enumerate(rows)]
        for n, row in enumerate(rows):
            row_b[at][n] = row
        each_chip(
            functools.partial(
                send, row_b[at], all_b[at].at[here], send_b.at[at], recv_b.at[at]
            )
        )
        for n, row in enumerate(rows):
            all_b[at][here, n] = row

    def finish_gather(at):
        wait_for(all_b[at].at[0 : CHIPS - 1], recv_b.at[at])
        return [
            jnp.sum(all_b[at][:, n].reshape(4, DOM, 128), axis=0)
            for n in range(all_b[at].shape[1])
        ]

    def start_halo(at, which, own):
        t = block_sum(own, mask)
        field[at] = t
        y_up[at, 0:3] = t[21:24]
        y_up[at, 3:5] = t[11:13]
        y_up[at, 5:7] = t[16:18]
        y_down[at, 0:3] = t[18:21]
        y_down[at, 3:5] = t[11:13]
        y_down[at, 5:7] = t[16:18]
        ss, rs = send_h.at[which], recv_h.at[which]
        send(field.at[at, 8:13], got_x.at[at, 0], ss.at[0], rs.at[0], (dom_prev, sub))
        send(field.at[at, 13:18], got_x.at[at, 1], ss.at[0], rs.at[0], (dom_next, sub))
        send(y_down.at[at], got_y.at[at, 0], ss.at[1], rs.at[1], (dom, sub_prev))
        send(y_up.at[at], got_y.at[at, 1], ss.at[1], rs.at[1], (dom, sub_next))
        for n, where in enumerate(diagonals):
            src = field.at[at, 11:13] if n < 2 else field.at[at, 16:18]
            send(src, got_c.at[at, n], ss.at[2], rs.at[2], where)
        return t

    def finish_halo(at, which, t):
        rs = recv_h.at[which]
        wait_for(got_x.at[at], rs.at[0])
        wait_for(got_y.at[at], rs.at[1])
        wait_for(got_c.at[at], rs.at[2])
        got = (
            got_x[at, 0],
            got_x[at, 1],
            got_y[at, 0],
            got_y[at, 1],
            [got_c[at, n] for n in range(4)],
        )
        return add_neighbours(t, got, mask, has)

    def apply(u):
        v = flat(u)
        g = product(need("cls_hi"), need("cls_lo"), v)
        h = pad_rows(g * weight_ref[...], 768)
        return cube(product(need("back_hi"), need("back_lo"), h) + need("react")[...] * v)

    def inner(a, b):
        return jnp.sum(a * b, axis=0, keepdims=True)

    def results(everyone, dots):
        rows = cube(everyone)
        terms = [
            jnp.sum(rows * cube(solve_ref[a]), axis=0, keepdims=True) for a in range(NFACE)
        ]
        column = jnp.sum(rows, axis=0, keepdims=True)
        which = lax.broadcasted_iota(jnp.int32, (1, 8, 128), 2) % 16
        terms += [jnp.where(which == NFACE + d, column, 0.0) for d in range(dots)]
        sums = jnp.sum(
            jnp.sum(jnp.concatenate(terms, axis=0), axis=1, keepdims=True), axis=2, keepdims=True
        )
        return [sums[n] for n in range(NFACE + dots)]

    pl.semaphore_wait(barrier, CHIPS - 1 + 2 + 4)
    rows = [packed(coarse_parts(by_kind(rhs_own)))]
    start_gather(0, rows)
    weighted = need("mass")[...] * move_lanes(pad_rows(need("visc")[...], ROWS), select, True)
    weight_ref[...] = jnp.concatenate([weighted, weighted, weighted], axis=0)
    diag_own = cube(need("react")[...] + product(need("sq_hi"), need("sq_lo"), weighted))
    forward_gather(0, rows)
    rhs_block = start_halo(0, 0, rhs_own)
    diag_block = start_halo(1, 1, diag_own)

    chosen = []
    for ax in (-1, 0, 1):
        for ay in (-1, 0, 1):
            at = jnp.clip((dom + ax) * SUB + sub + ay, 0, DOM * SUB - 1)
            chosen.append(need("coarse")[pl.ds(at, 1), :])
    for a in range(NFACE):
        wide = jnp.concatenate([need("place")[fx] * chosen[a] for fx in range(3)], axis=1)
        solve_ref[a] = sum(dot(piece, need("spread")[...]) for piece in thirds(wide))
    coarse_hi[...], coarse_lo[...] = halves(need("coarse")[...])

    for fx in range(3):
        for fy in range(3):
            phi_ref[3 * fx + fy] = from_kinds(along_x[fx] * along_y[fy])
    need("cls_hi"), need("cls_lo"), need("back_hi"), need("back_lo")

    def coarse_entries(first, last):
        @pl.loop(first, last)
        def _(f):
            entry_ref[f] = jnp.concatenate(coarse_parts(by_kind(apply(phi_ref[f]))), axis=0)

    coarse_entries(0, 5)
    r_all = finish_halo(0, 0, rhs_block)
    d_all = finish_halo(1, 1, diag_block)
    inverse = 1.0 / (d_all + cube(need("pad")[...]))
    solved = results(finish_gather(0)[0], 0)
    z0 = inverse * r_all + spread_coarse(solved)

    w0 = apply(z0)
    rows = [
        packed(coarse_parts(by_kind(w0)) + [inner(z0, rhs_own), inner(z0, w0)])
    ]
    start_gather(1, rows)
    w_block = start_halo(2, 2, w0)
    forward_gather(1, rows)
    coarse_entries(5, NFACE)
    sums = jnp.sum(jnp.sum(entry_ref[...].reshape(81, 8, 128), axis=1), axis=1, keepdims=True)
    sums = jnp.concatenate([sums, jnp.zeros((7, 1), F32)], axis=0)
    lanes = lax.broadcasted_iota(jnp.int32, (88, 128), 1)
    rows = [
        jnp.sum(
            jnp.where(lanes == 16 * sub + need("slots")[n], sums, 0.0), axis=0, keepdims=True
        )
        for n in range(2)
    ]
    start_gather(2, rows)
    forward_gather(2, rows)
    w0_all = finish_halo(2, 2, w_block)
    got = results(finish_gather(1)[0], 2)
    gamma0 = got[NFACE]
    alpha0 = gamma0 / got[NFACE + 1]
    m0 = inverse * w0_all + spread_coarse(got[:NFACE])
    z1 = z0 - alpha0 * m0
    r1 = rhs_own - alpha0 * w0

    w1 = apply(z1)
    w_block = start_halo(3, 3, w1)
    parts = coarse_parts(by_kind(w1)) + [
        inner(z1, r1),
        inner(z1, w1),
        inner(z1, w0),
        inner(m0, w1),
        inner(m0, w0),
    ]
    y = inverse * finish_halo(3, 3, w_block)
    t = apply(y)
    rows = [
        packed(parts + [inner(y, w1), inner(y, t)]),
        packed(coarse_parts(by_kind(t))),
    ]
    start_gather(3, rows)
    forward_gather(3, rows)
    entries = finish_gather(2)
    place = jnp.concatenate([need("place")[fx] for fx in range(3)], axis=1)
    every_w, every_t = finish_gather(3)
    got = results(every_w, 7)
    gamma1, z1w1, z1w0, m0w1, m0w0, yw1, yt = got[NFACE:]

    folded = lax.dot_general(
        jnp.concatenate(thirds(every_w), axis=0),
        need("spread")[...],
        (((1,), (1,)), ((), ())),
        preferred_element_type=F32,
    )
    folded = folded[:DOM] + folded[DOM : 2 * DOM] + folded[2 * DOM :]
    folded = jnp.sum(folded * place, axis=0, keepdims=True)
    folded = folded[:, :256] + folded[:, 256:512] + folded[:, 512:]
    high, low = halves(jnp.concatenate([folded, jnp.zeros((15, 256), F32)], axis=0))
    second = (
        dot(high, coarse_hi[...]) + dot(high, coarse_lo[...]) + dot(low, coarse_hi[...])
    )[0:1]
    wide = place * jnp.concatenate([second, second, second], axis=1)
    unfolded = dot(jnp.concatenate(thirds(wide), axis=0), need("unfold")[...])
    unfolded = unfolded[:DOM] + unfolded[DOM : 2 * DOM] + unfolded[2 * DOM :]
    chat = unfolded[:, :128]
    quad = sum(
        unfolded[:, 128 * (1 + n) : 128 * (2 + n)]
        * unfolded[:, 128 * (3 + n) : 128 * (4 + n)]
        * entries[n]
        for n in range(2)
    )

    def total(x):
        return jnp.sum(jnp.sum(x, axis=0, keepdims=True), axis=1, keepdims=True)

    m1w1 = yw1 + total(chat * every_w)
    m1am1 = yt + total(2.0 * (chat * every_t) + quad)
    beta0 = gamma1 / gamma0
    alpha1 = gamma1 / (z1w1 - beta0 * gamma1 / alpha0)
    gamma2 = (
        gamma1
        - 2.0 * alpha1 * (z1w1 + beta0 * z1w0)
        + alpha1 * alpha1 * (m1w1 + beta0 * (2.0 * m0w1 + beta0 * m0w0))
    )
    curve2 = (
        z1w1
        - 2.0 * alpha1 * (m1w1 + beta0 * m0w1)
        + alpha1
        * alpha1
        * (m1am1 + beta0 / alpha0 * (2.0 * (m0w1 - m1w1) + beta0 * (m0w0 - m0w1)))
    )
    beta1 = gamma2 / gamma1
    alpha2 = gamma2 / (curve2 - beta1 * gamma2 / alpha1)
    z2 = z1 - alpha1 * (y + spread_coarse(got[:NFACE]) + beta0 * m0)
    p1 = z1 + beta0 * z0
    q = alpha0 * z0 + alpha1 * p1 + alpha2 * (z2 + beta1 * p1)

    slots = pad_rows(move_lanes(flat(q), select, False), 256)
    press_ref[...] = sum(dot(need("out_pick")[...], piece) for piece in thirds(slots))[:NAT]
    grads = product(need("cls_hi"), need("cls_lo"), slots)
    for c in range(3):
        lin_ref[c] = lin_ref[c] - grads[ROWS * c : ROWS * c + NAT]

    for at in range(4):
        wait_for(all_a[at], send_a.at[at])
        wait_for(all_b[at].at[0 : CHIPS - 1], send_b.at[at])
        wait_for(got_x.at[at], send_h.at[at, 0])
        wait_for(got_y.at[at], send_h.at[at, 1])
        wait_for(got_c.at[at], send_h.at[at, 2])


def shards(velocity, base_flow, viscosity, cell_order, coarse_inv):
    args = [velocity, base_flow, viscosity, cell_order, coarse_inv]
    args += [jnp.asarray(t) for t in tables()]
    vmem = pl.BlockSpec(memory_space=pltpu.VMEM)
    hbm = pl.BlockSpec(memory_space=pltpu.HBM)
    dma = pltpu.SemaphoreType.DMA
    return pl.pallas_call(
        kernel,
        out_shape=(
            pltpu.VMEM((3, NAT, 128), F32),
            pltpu.VMEM((NAT, 128), F32),
        ),
        in_specs=[hbm] * len(args),
        out_specs=(vmem, vmem),
        scratch_shapes=[pltpu.VMEM(arg.shape, arg.dtype) for arg in args]
        + [
            dma((len(args),)),
            pltpu.VMEM((4, 28, 8, 128), F32),
            pltpu.VMEM((4, 7, 8, 128), F32),
            pltpu.VMEM((4, 7, 8, 128), F32),
            pltpu.VMEM((4, 2, 5, 8, 128), F32),
            pltpu.VMEM((4, 2, 7, 8, 128), F32),
            pltpu.VMEM((4, 4, 2, 8, 128), F32),
        ]
        + 3 * [pltpu.VMEM((n, 1, 128), F32) for n in MESSAGE_ROWS]
        + [pltpu.VMEM((CHIPS, n, 1, 128), F32) for n in MESSAGE_ROWS]
        + [
            pltpu.VMEM((3 * ROWS, 128), F32),
            pltpu.VMEM((NFACE, DOM, 128), F32),
            pltpu.VMEM((NFACE, 28, 8, 128), F32),
            pltpu.VMEM((NFACE, NFACE, 8, 128), F32),
            pltpu.VMEM((256, 256), BF16),
            pltpu.VMEM((256, 256), BF16),
            dma((4, 3)),
            dma((4, 3)),
            dma((4,)),
            dma((4,)),
            dma((4,)),
            dma((4,)),
        ],
        compiler_params=pltpu.CompilerParams(
            collective_id=0, has_side_effects=True, vmem_limit_bytes=40 << 20
        ),
    )(*[pltpu.with_memory_space_constraint(arg, pltpu.HBM) for arg in args])


def solution(mesh):
    placed = (
        P(None, None, ("dom", "sub")),
        P(None, None, ("dom", "sub")),
        P(None, ("dom", "sub")),
        P(("dom", "sub"), None),
        P(),
    )
    return jax.shard_map(
        shards,
        mesh=mesh,
        in_specs=placed,
        out_specs=(P(None, None, ("dom", "sub")), P(None, ("dom", "sub"))),
        check_vma=False,
    )
```
